512 devices in a mesh: ctx: 64 (over x, z, core), head: 8 (over y).
Axes of the slice: x: 4, y: 8, z: 8, core: 2. Of those that a mesh axis runs over, the one named last changes fastest.
Arguments:
- xin: bfloat16 [16384, 4096], P('ctx', 'head'), may hold values from -6 to 6
- zin: bfloat16 [16384, 4096], P('ctx', 'head'), may hold values from -6 to 6
- bmat: bfloat16 [16384, 128], P('ctx'), may hold values from -6 to 6
- cmat: bfloat16 [16384, 128], P('ctx'), may hold values from -6 to 6
- ldec: float32 [64, 16384], P('head', 'ctx'), may hold values from -1 to 0, as said below
- dskip: float32 [64], P('head'), may hold values from 0.5 to 2
- gain: float32 [4096], P('head'), may hold values from 0.1 to 1.9
- w_out: bfloat16 [2048, 4096], P('ctx', 'head'), may hold values from -0.09375 to 0.09375
- dout: bfloat16 [16384, 2048], P('ctx', 'head'), may hold values from -16 to 16
Outputs:
- grad_x: bfloat16 [16384, 4096], P('ctx', 'head')
- grad_z: bfloat16 [16384, 4096], P('ctx', 'head')
- grad_b: float32 [16384, 128], P('ctx')
- grad_c: float32 [16384, 128], P('ctx')
- grad_w: float32 [2048, 4096], P('ctx', 'head')
- grad_gain: float32 [4096], P('head')
- grad_skip: float32 [64], P('head')
The draws below stay inside these ranges and needn't reach their ends.
Inputs may be any that keep to these rules, and one draw needn't show every extreme that they name: `ldec`: every entry is at most zero.
All inputs are finite; a program needn't handle non-finite values.
Results may differ from the reference program's by a relative error of at most 0.0015.
Values may be sent and summed in bfloat16 or wider, within the bound.
A program may use at most 128 MiB of HBM per device.

```python
import math
import jax
import jax.numpy as jnp
from jax import lax

WIDTH = 2048
HEADS = 64
HDIM = 64
STATE = 128
TOK_DEV = 256
INNER = 4096
SEQUENCE_LENGTH = 16384


def draw_ldec(key, part):
    keys = jax.random.split(jax.random.fold_in(key, 11), 4)
    share = 0.5
    quick = jax.random.uniform(keys[0], (HEADS, 1)) < share
    initial_position = jnp.where(quick, 1.0 / 40.0, 0.5 / SEQUENCE_LENGTH)
    approximate_guess = jax.random.uniform(keys[1], (HEADS, SEQUENCE_LENGTH), minval=0.5, maxval=2.0)
    element_locations = jax.random.randint(keys[2], (3,), 0, SEQUENCE_LENGTH)
    element_group = jnp.any(jnp.arange(SEQUENCE_LENGTH)[None, :] == element_locations[:, None], axis=0).astype(jnp.float32)
    level_index = jax.random.uniform(keys[3], (HEADS, 1), minval=0.2, maxval=0.5)
    return (-(initial_position * approximate_guess + element_group[None, :] * level_index)).astype(jnp.float32)


def spiked(entries, key, source, target, blocks, factor):
    owner, partner = [(jnp.arange(entries.shape[axis_at]) // (entries.shape[axis_at] // blocks)).reshape([-1 if axis == axis_at else 1 for axis in range(entries.ndim)]) for axis_at in (source, target)]
    chosen = jax.random.permutation(key, blocks)[partner]
    strong = (owner == chosen) | (owner == (partner + blocks // 2) % blocks)
    return jnp.where(strong, factor * entries, entries)


def shard_levels(rng, dims, pieces, low, high):
    factor_of, own = 1.0, jax.random.fold_in(rng, 6)
    for dim, shards_of in pieces:
        draws = jnp.exp(jax.random.uniform(jax.random.fold_in(own, dim), (shards_of,), jnp.float32, low / len(pieces), high / len(pieces)))
        factor_of = factor_of * jnp.repeat(draws, dims[dim] // shards_of).reshape([-1 if axis == dim else 1 for axis in range(len(dims))])
    return factor_of


def normal_values(stream_key, extent, scale, most, shards=(), held_as=jnp.bfloat16):
    values = jax.random.normal(stream_key, extent, jnp.float32) * scale
    if len(shards) > 0:
        values = shard_levels(stream_key, extent, shards, -0.22, 0.18) * values
    return jnp.clip(values, min=-most, max=most).astype(held_as)


def bell_draw_with(key, dims, width, reach, cuts, heavy, kind=jnp.bfloat16):
    array = width * jax.random.normal(key, dims, jnp.float32)
    if cuts:
        array = array * shard_levels(key, dims, cuts, -0.22, 0.18)
    return jnp.clip(spiked(array, jax.random.fold_in(key, 3), *heavy), -reach, reach).astype(kind)


def setup_inputs(seed: int = 0) -> dict:
    key_list = jax.random.split(jax.random.key(seed), 10)
    return {
        "xin": normal_values(key_list[0], (SEQUENCE_LENGTH, INNER), 1.0, 6.0, ((0, 64), (1, 8))),
        "zin": normal_values(key_list[1], (SEQUENCE_LENGTH, INNER), 1.0, 6.0, ((0, 64), (1, 8))),
        "bmat": normal_values(key_list[2], (SEQUENCE_LENGTH, STATE), 1.0, 6.0, ((0, 64),)),
        "cmat": normal_values(key_list[3], (SEQUENCE_LENGTH, STATE), 1.0, 6.0, ((0, 64),)),
        "ldec": draw_ldec(jax.random.fold_in(key_list[9], 71), 0),
        "dskip": jnp.clip(jnp.exp(math.log(2.0) - 1.3862944 * jax.random.uniform(key_list[5], (HEADS,), jnp.float32) ** shard_levels(key_list[5], (HEADS,), ((0, 8),), -0.2, 0.2)), 0.5, 2.0),
        "gain": jnp.clip(1.0 + 0.18 * jax.random.normal(key_list[6], (INNER,), jnp.float32), 0.1, 1.9),
        "w_out": normal_values(key_list[7], (WIDTH, INNER), INNER ** -0.5, 0.09375, ((0, 64), (1, 8))),
        "dout": bell_draw_with(key_list[8], (SEQUENCE_LENGTH, WIDTH), 1.0, 16.0, ((0, 64), (1, 8)), (0, 1, 64, 4.0)),
    }


HIGH = lax.Precision.HIGHEST
EPSILON = 1e-05

def mixer_norm(values_x, values_z, values_b, values_c, gain_vec, skip_vec, logdec):
    blocks = SEQUENCE_LENGTH // TOK_DEV
    xs = values_x.reshape(blocks, TOK_DEV, HEADS, HDIM)
    bs = values_b.reshape(blocks, TOK_DEV, STATE)
    cs = values_c.reshape(blocks, TOK_DEV, STATE)
    ls = logdec.reshape(HEADS, blocks, TOK_DEV).transpose(1, 0, 2)
    positions = jnp.arange(TOK_DEV)
    causal = positions[:, None] >= positions[None, :]

    def step_forward(state, inputs):
        block_x, block_b, block_c, block_l = inputs
        cumlog = jnp.cumsum(block_l, axis=1)
        gaps = cumlog[:, :, None] - cumlog[:, None, :]
        decays = jnp.where(causal[None], jnp.exp(jnp.where(causal[None], gaps, 0.0)), 0.0)
        scores = jnp.dot(block_c, block_b.T, precision=HIGH)
        inner_out = jnp.einsum('hts,shp->thp', decays * scores[None], block_x, precision=HIGH)
        carried = jnp.einsum('hpn,tn->thp', state, block_c, precision=HIGH) * jnp.exp(cumlog).T[:, :, None]
        tail = jnp.exp(cumlog[:, -1:] - cumlog)
        fresh = jnp.einsum('ht,thp,tn->hpn', tail, block_x, block_b, precision=HIGH)
        new_state = state * jnp.exp(cumlog[:, -1])[:, None, None] + fresh
        return (new_state, inner_out + carried)
    start = jnp.zeros((HEADS, HDIM, STATE), jnp.float32)
    _, outputs = lax.scan(step_forward, start, (xs, bs, cs, ls))
    mixed = outputs.reshape(SEQUENCE_LENGTH, HEADS, HDIM) + skip_vec[None, :, None] * values_x.reshape(SEQUENCE_LENGTH, HEADS, HDIM)
    mixed = mixed.reshape(SEQUENCE_LENGTH, INNER)
    gated = mixed * values_z * jax.nn.sigmoid(values_z)
    inv_rms = lax.rsqrt(lax.optimization_barrier(jnp.mean(gated * gated, axis=1, keepdims=True)) + EPSILON)
    return gated * inv_rms * gain_vec

def reference(xin, zin, bmat, cmat, ldec, dskip, gain, w_out, dout):

    def forward(values_x, values_z, values_b, values_c, gain_vec, skip_vec):
        return mixer_norm(values_x, values_z, values_b, values_c, gain_vec, skip_vec, ldec)
    normed, pullback = jax.vjp(forward, xin.astype(jnp.float32), zin.astype(jnp.float32), bmat.astype(jnp.float32), cmat.astype(jnp.float32), gain, dskip)
    normed_grad = jnp.dot(dout, w_out, preferred_element_type=jnp.float32)
    grad_w = lax.dot_general(dout.astype(jnp.float32), normed, (((0,), (0,)), ((), ())), precision=HIGH, preferred_element_type=jnp.float32)
    grad_x, grad_z, grad_b, grad_c, grad_gain, grad_skip = pullback(normed_grad)
    return (grad_x.astype(jnp.bfloat16), grad_z.astype(jnp.bfloat16), grad_b, grad_c, grad_w, grad_gain, grad_skip)
```

```python
import functools
import jax
import jax.numpy as jnp
from jax import lax
from jax.experimental import pallas as pl
from jax.experimental.pallas import tpu as pltpu
from jax.sharding import PartitionSpec as P

HDIM = 64
HIGH = lax.Precision.HIGHEST
EPSILON = 1e-05
MESH = pl.DeviceIdType.MESH
NX, NZ, NC = 4, 8, 2
VMEM_LIMIT = 48 * 2**20


def remote(src, dst, sent, came, **where):
    return pltpu.make_async_remote_copy(
        src_ref=src, dst_ref=dst, send_sem=sent, recv_sem=came, device_id=where, device_id_type=MESH
    )


def wait_for(ref, sem):
    pltpu.make_async_copy(ref, ref, sem).wait()


def others(axis, act):
    count, mine = lax.axis_size(axis), lax.axis_index(axis)

    def turn(step, carry):
        act(lax.rem(mine + step, count))
        return carry

    lax.fori_loop(1, count, turn, 0)


def greet(*axes):
    barrier = pltpu.get_barrier_semaphore()
    total = 0
    for axis in axes:
        others(
            axis,
            lambda peer: pl.semaphore_signal(
                barrier, inc=1, device_id={axis: peer}, device_id_type=MESH
            ),
        )
        total += lax.axis_size(axis) - 1
    pl.semaphore_wait(barrier, total)


def coordinates():
    mine = lax.axis_index("ctx")
    return mine // (NZ * NC), lax.rem(mine // NC, NZ), lax.rem(mine, NC)


def ctx_of(x, z, core):
    return (x * NZ + z) * NC + core


def scan_send(local, got, sent, came):
    mine = lax.axis_index("ctx")
    rows = got.shape[1]

    def part(index):
        return local.at[pl.ds(pl.multiple_of(index * rows, rows), rows)]

    others("ctx", lambda peer: remote(part(peer), got.at[mine], sent, came, ctx=peer).start())
    pltpu.make_async_copy(part(mine), got.at[mine], came).start()


def scan_turn(got, decays, before, out, sent, came, came_back, backward):
    mine = lax.axis_index("ctx")
    count, rows = got.shape[0], got.shape[1]
    wait_for(got, came)

    def turn(step, total):
        index = count - 1 - step if backward else step
        before[index] = total
        return decays[index] * total + got[index]

    lax.fori_loop(0, count, turn, jnp.zeros(got.shape[1:], jnp.float32))
    home = out.at[pl.ds(pl.multiple_of(mine * rows, rows), rows)]
    others("ctx", lambda peer: remote(before.at[peer], home, sent, came_back, ctx=peer).start())
    pltpu.make_async_copy(before.at[mine], home, came_back).start()


def scan_end(got, out, sent, sent_back, came_back):
    count = got.shape[0]
    wait_for(out, came_back)
    wait_for(got.at[pl.ds(0, count - 1)], sent)
    wait_for(got.at[pl.ds(0, count - 1)], sent_back)


def first_kernel(
    state, decay, w_mine, dout_mine, came_in, decays, w_all, dout_all,
    got, before, state_sems, decay_sems, w_sent, w_z, w_x, w_core, w_own, d_sent, d_came,
):
    greet("ctx", "head")
    mine, row = lax.axis_index("ctx"), lax.axis_index("head")
    count, rows_count = lax.axis_size("ctx"), lax.axis_size("head")
    x, z, core = coordinates()
    slice_rows = got.shape[1]
    heads_per = HDIM // slice_rows
    others(
        "ctx",
        lambda peer: remote(
            decay.at[peer // heads_per], decays.at[mine], decay_sems.at[0], decay_sems.at[1], ctx=peer
        ).start(),
    )
    pltpu.make_async_copy(decay.at[mine // heads_per], decays.at[mine], decay_sems.at[1]).start()
    scan_send(state, got, state_sems.at[0], state_sems.at[1])
    w_home = pltpu.make_async_copy(w_mine, w_all.at[x, z, core], w_own)
    w_home.start()
    for step in range(1, NZ):
        peer = lax.rem(z + step, NZ)
        remote(w_mine, w_all.at[x, z, core], w_sent, w_z.at[step], ctx=ctx_of(x, peer, core)).start()
    right, left = lax.rem(row + 1, rows_count), lax.rem(row + rows_count - 1, rows_count)
    far, near = rows_count // 2, rows_count - 1 - rows_count // 2

    def ring(step):
        if step < far:
            piece = lax.rem(row + rows_count - step, rows_count)
            source = dout_mine if step == 0 else dout_all.at[piece]
            if step:
                wait_for(dout_all.at[piece], d_came.at[0, step])
            remote(source, dout_all.at[piece], d_sent, d_came.at[0, step + 1], head=right).start()
        if step < near:
            piece = lax.rem(row + step, rows_count)
            source = dout_mine if step == 0 else dout_all.at[piece]
            if step:
                wait_for(dout_all.at[piece], d_came.at[1, step])
            remote(source, dout_all.at[piece], d_sent, d_came.at[1, step + 1], head=left).start()

    ring(0)
    for step in range(NX - 1):
        peer = lax.rem(x + step + 1, NX)
        remote(
            w_mine, w_all.at[x, z, core], w_sent, w_x.at[step], ctx=ctx_of(peer, z, core)
        ).start()
    for step in range(1, NZ):
        source = lax.rem(z + NZ - step, NZ)
        wait_for(w_all.at[x, source, core], w_z.at[step])
        for turn in range(NX - 1):
            peer = lax.rem(x + turn + 1, NX)
            remote(
                w_all.at[x, source, core], w_all.at[x, source, core], w_sent, w_x.at[turn],
                ctx=ctx_of(peer, z, core),
            ).start()
    w_home.wait()
    twin = ctx_of(x, z, 1 - core)
    remote(w_all.at[x, :, core], w_all.at[x, :, core], w_sent, w_core.at[0], ctx=twin).start()
    wait_for(decays, decay_sems.at[1])
    scan_turn(
        got, decays, before, came_in, state_sems.at[2], state_sems.at[1], state_sems.at[3], False
    )
    for step in range(1, far):
        ring(step)
    for turn in range(NX - 1):
        source = lax.rem(x + NX - turn - 1, NX)
        wait_for(w_all.at[source, :, core], w_x.at[turn])
        remote(
            w_all.at[source, :, core], w_all.at[source, :, core], w_sent, w_core.at[turn + 1], ctx=twin
        ).start()
    dout_all[row] = dout_mine[...]
    wait_for(dout_all.at[lax.rem(row + rows_count - far, rows_count)], d_came.at[0, far])
    if near:
        wait_for(dout_all.at[lax.rem(row + near, rows_count)], d_came.at[1, near])
    for turn in range(NX):
        source = lax.rem(x + NX - turn, NX)
        wait_for(w_all.at[source, :, 1 - core], w_core.at[turn])
    scan_end(got, came_in, state_sems.at[0], state_sems.at[2], state_sems.at[3])
    wait_for(decays.at[pl.ds(0, count - 1)], decay_sems.at[0])
    wait_for(dout_all.at[pl.ds(0, rows_count - 1)], d_sent)
    for turn in range(NX):
        wait_for(w_all.at[turn, :, 0], w_sent)
    for turn in range(NX - 1):
        wait_for(w_all.at[turn, :, 0], w_sent)
    wait_for(w_all.at[0, pl.ds(0, NZ - 1), 0], w_sent)


def sum_kernel(part, total, got, sent, came):
    greet("head")
    mine, count = lax.axis_index("head"), lax.axis_size("head")
    others("head", lambda peer: remote(part, got.at[mine], sent, came, head=peer).start())
    pltpu.make_async_copy(part, got.at[mine], came).start()
    wait_for(got, came)
    value = got[0]
    for index in range(1, count):
        value = value + got[index]
    total[...] = value
    wait_for(got.at[pl.ds(0, count - 1)], sent)


def shared_kernel(part, total, got, summed, sems):
    greet("head")
    mine, count = lax.axis_index("head"), lax.axis_size("head")
    rows = got.shape[1]

    def at(ref, index):
        return ref.at[pl.ds(pl.multiple_of(index * rows, rows), rows)]

    others(
        "head", lambda peer: remote(at(part, peer), got.at[mine], sems.at[0], sems.at[1], head=peer).start()
    )
    pltpu.make_async_copy(at(part, mine), got.at[mine], sems.at[1]).start()
    wait_for(got, sems.at[1])
    value = got[0]
    for index in range(1, count):
        value = value + got[index]
    summed[...] = value
    others(
        "head", lambda peer: remote(summed, at(total, mine), sems.at[2], sems.at[3], head=peer).start()
    )
    pltpu.make_async_copy(summed, at(total, mine), sems.at[3]).start()
    wait_for(total, sems.at[3])
    wait_for(got.at[pl.ds(0, count - 1)], sems.at[0])
    wait_for(got.at[pl.ds(0, count - 1)], sems.at[2])


PARTS = 2


def second_kernel(
    state, decays, grads, gains, came_in, grad, gain_total,
    got, before, twin_got, mid, x_got, low, z_got, gains_got,
    state_sems, gain_sems, twin_sems, x_sent, x_came, z_sent, z_came,
):
    greet("ctx")
    mine, count = lax.axis_index("ctx"), lax.axis_size("ctx")
    x, z, core = coordinates()
    twin = ctx_of(x, z, 1 - core)
    depth = NZ // PARTS
    order = [lax.rem(x + step, NX) for step in range(1, NX + 1)]
    scan_send(state, got, state_sems.at[0], state_sems.at[1])
    for step in range(NX):
        remote(
            grads.at[order[step], :, 1 - core], twin_got.at[order[step]], twin_sems.at[0, step],
            twin_sems.at[1, step], ctx=twin,
        ).start()
    others(
        "ctx", lambda peer: remote(gains, gains_got.at[mine], gain_sems.at[0], gain_sems.at[1], ctx=peer).start()
    )
    pltpu.make_async_copy(gains, gains_got.at[mine], gain_sems.at[1]).start()
    for step in range(NX):
        wait_for(twin_got.at[order[step]], twin_sems.at[1, step])

        def add(index, carry):
            mid[order[step], index] = (
                grads[order[step], index, core] + twin_got[order[step], index]
            )
            return carry

        lax.fori_loop(0, NZ, add, 0)
        if step < NX - 1:
            for part in range(PARTS):
                block = pl.ds(part * depth, depth)
                remote(
                    mid.at[order[step], block], x_got.at[step, block], x_sent, x_came.at[part, step],
                    ctx=ctx_of(order[step], z, core),
                ).start()
    scan_turn(
        got, decays, before, came_in, state_sems.at[2], state_sems.at[1], state_sems.at[3], True
    )
    for part in range(PARTS):
        block = pl.ds(part * depth, depth)
        for step in range(NX - 1):
            wait_for(x_got.at[step, block], x_came.at[part, step])

        def fold(turn, carry):
            index = lax.rem(z + turn + 1, NZ)

            @pl.when((index >= part * depth) & (index < (part + 1) * depth))
            def _():
                value = mid[x, index]
                for step in range(NX - 1):
                    value = value + x_got[step, index]
                low[index] = value

                @pl.when(index != z)
                def _():
                    remote(
                        low.at[index], z_got.at[z], z_sent, z_came, ctx=ctx_of(x, index, core)
                    ).start()

            return carry

        lax.fori_loop(0, NZ, fold, 0)
    pltpu.make_async_copy(low.at[z], z_got.at[z], z_came).start()
    wait_for(gains_got, gain_sems.at[1])
    gain_total[...] = lax.fori_loop(
        1, count, lambda index, value: value + gains_got[index], gains_got[0]
    )
    wait_for(z_got, z_came)
    value = z_got[0]
    for index in range(1, NZ):
        value = value + z_got[index]
    grad[...] = value
    scan_end(got, came_in, state_sems.at[0], state_sems.at[2], state_sems.at[3])
    wait_for(gains_got.at[pl.ds(0, count - 1)], gain_sems.at[0])
    for step in range(NX):
        wait_for(twin_got.at[step], twin_sems.at[0, step])
    for step in range(NX - 1):
        wait_for(x_got.at[step], x_sent)
    wait_for(z_got.at[pl.ds(0, NZ - 1)], z_sent)


def call(kernel, outs, scratch, ident, *operands):
    vmem = pl.BlockSpec(memory_space=pltpu.VMEM)
    return pl.pallas_call(
        kernel,
        out_shape=outs,
        in_specs=[vmem] * len(operands),
        out_specs=jax.tree.map(lambda _: vmem, outs),
        scratch_shapes=scratch,
        compiler_params=pltpu.CompilerParams(
            collective_id=ident, has_side_effects=True, vmem_limit_bytes=VMEM_LIMIT
        ),
    )(*operands)


def per_device(xin, zin, bmat, cmat, ldec, dskip, gain, w_out, dout):
    f32, bf16 = jnp.float32, jnp.bfloat16
    shape = jax.ShapeDtypeStruct
    dma = pltpu.SemaphoreType.DMA
    blocks, groups = lax.axis_size("ctx"), lax.axis_size("head")
    heads_here, tokens = ldec.shape
    states, width = heads_here * HDIM, bmat.shape[1]
    rows = states // blocks
    inner = xin.shape[1]
    values_x = xin.astype(f32).reshape(tokens, heads_here, HDIM)
    values_b = bmat.astype(f32)
    values_c = cmat.astype(f32)
    positions = jnp.arange(tokens)
    causal = positions[:, None] >= positions[None, :]
    cumlog = jnp.dot(ldec, causal.T.astype(f32), precision=HIGH)
    tail = jnp.exp(cumlog[:, -1:] - cumlog)
    increasing_order = jnp.exp(cumlog)
    local_state = jnp.einsum("ht,thp,tn->hpn", tail, values_x, values_b, precision=HIGH)
    total_decay = jnp.exp(cumlog[:, -1])
    came_in, decays, w_all, dout_all = call(
        first_kernel,
        (
            shape((states, width), f32),
            shape((blocks, 1, width), f32),
            shape((NX, NZ, NC) + w_out.shape, bf16),
            shape((groups,) + dout.shape, bf16),
        ),
        [
            pltpu.VMEM((blocks, rows, width), f32),
            pltpu.VMEM((blocks, rows, width), f32),
            dma((4,)), dma((2,)), dma(()), dma((NZ,)), dma((NX,)), dma((NX,)), dma(()), dma(()),
            dma((2, groups // 2 + 1)),
        ],
        0,
        local_state.reshape(states, width),
        jnp.broadcast_to(total_decay[:, None, None], (heads_here, 1, width)),
        w_out,
        dout,
    )
    incoming_hidden = came_in.reshape(heads_here, HDIM, width)
    columns = jnp.transpose(dout_all, (1, 0, 2)).reshape(tokens, -1)
    normed_grad = jnp.dot(columns, w_all.reshape(-1, inner), preferred_element_type=f32)
    gaps = cumlog[:, :, None] - cumlog[:, None, :]
    decay = jnp.where(causal[None], jnp.exp(jnp.where(causal[None], gaps, 0.0)), 0.0)
    scores = jnp.dot(values_c, values_b.T, precision=HIGH)
    kernel = decay * scores[None]
    inner_out = jnp.einsum("hts,shp->thp", kernel, values_x, precision=HIGH)
    carried = (
        jnp.einsum("hpn,tn->thp", incoming_hidden, values_c, precision=HIGH)
        * increasing_order.T[:, :, None]
    )
    mixed = inner_out + carried + dskip[None, :, None] * values_x
    mixed = mixed.reshape(tokens, -1)
    values_z = zin.astype(f32)
    sigmoid_z = jax.nn.sigmoid(values_z)
    gate_act = values_z * sigmoid_z
    gated = mixed * gate_act
    weighted = gain * normed_grad
    features_all = inner * groups
    sums = jnp.stack([jnp.sum(gated * gated, axis=1), jnp.sum(weighted * gated, axis=1)])
    sums = jnp.pad(sums, ((0, 6), (0, 0)))
    sums = call(
        sum_kernel, shape(sums.shape, f32), [pltpu.VMEM((groups,) + sums.shape, f32), dma(()), dma(())], 1, sums
    )
    inv_rms = lax.rsqrt(sums[0] / features_all + EPSILON)[:, None]
    inner_total = sums[1]
    normed = gated * inv_rms * gain
    gain_part = jnp.sum(normed_grad * gated * inv_rms, axis=0)
    gated_grad = (
        inv_rms * weighted
        - gated * (inv_rms * inv_rms * inv_rms) * (inner_total / features_all)[:, None]
    )
    mixed_grad = gated_grad * gate_act
    grad_z = gated_grad * mixed * sigmoid_z * (1.0 + values_z * (1.0 - sigmoid_z))
    head_grad = mixed_grad.reshape(tokens, heads_here, HDIM)
    skip_part = jnp.sum(head_grad * values_x, axis=(0, 2))
    local_grad = jnp.einsum("ht,thp,tn->hpn", increasing_order, head_grad, values_c, precision=HIGH)
    high = lax.reduce_precision(normed, 8, 7)
    low = (normed - high).astype(bf16)
    grads = lax.dot_general(
        columns, high.astype(bf16), (((0,), (0,)), ((), ())), preferred_element_type=f32
    ) + lax.dot_general(columns, low, (((0,), (0,)), ((), ())), preferred_element_type=f32)
    gain_rows = inner // 128
    small = jnp.concatenate(
        [
            gain_part.reshape(gain_rows, 128),
            jnp.pad(skip_part, (0, 128 - heads_here))[None],
            jnp.zeros((8 - gain_rows - 1, 128), f32),
        ]
    )
    out_rows = w_out.shape[0]
    piece = (out_rows, inner)
    grad_in, grad_w, small = call(
        second_kernel,
        (shape((states, width), f32), shape(piece, f32), shape(small.shape, f32)),
        [
            pltpu.VMEM((blocks, rows, width), f32),
            pltpu.VMEM((blocks, rows, width), f32),
            pltpu.VMEM((NX, NZ) + piece, f32),
            pltpu.VMEM((NX, NZ) + piece, f32),
            pltpu.VMEM((NX - 1, NZ) + piece, f32),
            pltpu.VMEM((NZ,) + piece, f32),
            pltpu.VMEM((NZ,) + piece, f32),
            pltpu.VMEM((blocks,) + small.shape, f32),
            dma((4,)), dma((2,)), dma((2, NX)), dma(()), dma((PARTS, NX)), dma(()), dma(()),
        ],
        2,
        local_grad.reshape(states, width),
        decays,
        grads.reshape((NX, NZ, NC) + piece),
        small,
    )
    grad_in = grad_in.reshape(heads_here, HDIM, width)
    products = jnp.einsum("thp,shp->hts", head_grad, values_x, precision=HIGH) * decay
    grad_x = jnp.einsum("hts,thp->shp", kernel, head_grad, precision=HIGH)
    grad_x = (
        grad_x + jnp.einsum("hpn,sn->shp", grad_in, values_b, precision=HIGH) * tail.T[:, :, None]
    )
    grad_x = grad_x + dskip[None, :, None] * head_grad
    products = jnp.sum(products, axis=0)
    grad_b = jnp.einsum("ts,tn->sn", products, values_c, precision=HIGH)
    grad_b = grad_b + jnp.einsum("hpn,shp,hs->sn", grad_in, values_x, tail, precision=HIGH)
    grad_c = jnp.einsum("ts,sn->tn", products, values_b, precision=HIGH)
    grad_c = grad_c + jnp.einsum(
        "hpn,thp,ht->tn", incoming_hidden, head_grad, increasing_order, precision=HIGH
    )
    shared = jnp.concatenate([grad_b, grad_c])
    share = (shared.shape[0] // groups, width)
    shared = call(
        shared_kernel,
        shape(shared.shape, f32),
        [pltpu.VMEM((groups,) + share, f32), pltpu.VMEM(share, f32), dma((4,))],
        3,
        shared,
    )
    return (
        grad_x.reshape(tokens, -1).astype(bf16),
        grad_z.astype(bf16),
        shared[:tokens],
        shared[tokens:],
        grad_w,
        small[:gain_rows].reshape(-1),
        small[gain_rows, :heads_here],
    )


def solution(mesh):
    return jax.shard_map(
        per_device,
        mesh=mesh,
        in_specs=(
            P("ctx", "head"), P("ctx", "head"), P("ctx", None), P("ctx", None), P("head", "ctx"),
            P("head"), P("head"), P("ctx", "head"), P("ctx", "head"),
        ),
        out_specs=(
            P("ctx", "head"), P("ctx", "head"), P("ctx", None), P("ctx", None), P("ctx", "head"),
            P("head"), P("head"),
        ),
        check_vma=False,
    )
```

```python
import types
import jax
import jax.numpy as jnp
from jax import lax
from jax.experimental import pallas as pl
from jax.experimental.pallas import tpu as pltpu
from jax.sharding import PartitionSpec as P

HDIM = 64
HIGH = lax.Precision.HIGHEST
EPSILON = 1e-05
MESH = pl.DeviceIdType.MESH
NX, NZ, NC = 4, 8, 2
PARTS = 2
LANES = 128
CHUNK = 16
VMEM_LIMIT = 56 * 2**20
f32, bf16 = jnp.float32, jnp.bfloat16


def remote(src, dst, sent, came, **where):
    return pltpu.make_async_remote_copy(
        src_ref=src, dst_ref=dst, send_sem=sent, recv_sem=came, device_id=where, device_id_type=MESH
    )


def local(src, dst, sem):
    return pltpu.make_async_copy(src, dst, sem)


def wait_for(ref, sem):
    local(ref, ref, sem).wait()


def others(axis, act):
    count, mine = lax.axis_size(axis), lax.axis_index(axis)

    def turn(step, carry):
        act(lax.rem(mine + step, count))
        return carry

    lax.fori_loop(1, count, turn, 0)


def ctx_of(x, z, core):
    return (x * NZ + z) * NC + core


def split(value):
    high = value.astype(bf16)
    return high, (value - high.astype(f32)).astype(bf16)


def dot(a, b):
    return jnp.dot(a, b, preferred_element_type=f32)


def dot_nt(a, b, precision=None):
    return lax.dot_general(
        a, b, (((1,), (1,)), ((), ())), preferred_element_type=f32, precision=precision
    )


def rows_at(ref, index, rows):
    return ref.at[pl.ds(pl.multiple_of(index * rows, rows), rows)]


def loop(count, body):
    def turn(index, carry):
        body(index)
        return carry

    lax.fori_loop(0, count, turn, 0)


def scan_send(state, got, sent, came):
    mine, rows = lax.axis_index("ctx"), got.shape[1]
    others(
        "ctx",
        lambda peer: remote(rows_at(state, peer, rows), got.at[mine], sent, came, ctx=peer).start(),
    )
    local(rows_at(state, mine, rows), got.at[mine], came).start()


def scan_turn(got, decays, before, out, sent, came, came_back, backward):
    mine = lax.axis_index("ctx")
    count, rows = got.shape[0], got.shape[1]
    head = mine // (HDIM // rows)
    wait_for(got, came)

    def turn(step, total):
        index = count - 1 - step if backward else step
        before[index] = total
        factor = decays[
            index // (NZ * NC), lax.rem(index // NC, NZ), lax.rem(index, NC), head
        ]
        return factor * total + got[index]

    lax.fori_loop(0, count, turn, jnp.zeros(got.shape[1:], f32), unroll=4)
    home = rows_at(out, mine, rows)
    others("ctx", lambda peer: remote(before.at[peer], home, sent, came_back, ctx=peer).start())
    local(before.at[mine], home, came_back).start()


def shared_send(part, got, sems):
    mine, rows = lax.axis_index("head"), got.shape[1]
    others(
        "head",
        lambda peer: remote(rows_at(part, peer, rows), got.at[mine], sems.at[0], sems.at[1], head=peer).start(),
    )
    local(rows_at(part, mine, rows), got.at[mine], sems.at[1]).start()


def shared_turn(got, summed, total, sems):
    mine, rows = lax.axis_index("head"), got.shape[1]
    wait_for(got, sems.at[1])
    value = got[0]
    for index in range(1, got.shape[0]):
        value = value + got[index]
    summed[...] = value
    home = rows_at(total, mine, rows)
    others("head", lambda peer: remote(summed, home, sems.at[2], sems.at[3], head=peer).start())
    local(summed, home, sems.at[3]).start()


def shared_end(got, total, sems):
    peers = got.at[pl.ds(0, got.shape[0] - 1)]
    wait_for(total, sems.at[3])
    wait_for(peers, sems.at[0])
    wait_for(peers, sems.at[2])


def whole_kernel(names, *refs):
    r = types.SimpleNamespace(**dict(zip(names, refs)))
    mine, row = lax.axis_index("ctx"), lax.axis_index("head")
    count, groups = lax.axis_size("ctx"), lax.axis_size("head")
    x, z, core = mine // (NZ * NC), lax.rem(mine // NC, NZ), lax.rem(mine, NC)
    twin = ctx_of(x, z, 1 - core)
    heads, tokens = r.ldec.shape
    pairs = heads // 2
    inner = heads * HDIM
    half = tokens // 2
    features = inner * groups
    chunks = tokens // CHUNK
    first_head = lax.broadcasted_iota(jnp.int32, (tokens, LANES), 1) < HDIM

    def pair_lanes(pair):
        return pl.ds(pl.multiple_of(pair * LANES, LANES), LANES)

    def chunk_rows(chunk):
        return pl.ds(pl.multiple_of(chunk * CHUNK, CHUNK), CHUNK)

    barrier = pltpu.get_barrier_semaphore()
    for axis in ("ctx", "head"):
        others(
            axis,
            lambda peer: pl.semaphore_signal(
                barrier, inc=1, device_id={axis: peer}, device_id_type=MESH
            ),
        )

    token_of = lax.broadcasted_iota(jnp.int32, (tokens, tokens), 0)
    other_of = lax.broadcasted_iota(jnp.int32, (tokens, tokens), 1)
    logs = dot_nt(r.ldec[...], (token_of >= other_of).astype(f32), HIGH)
    columns = jnp.transpose(logs)
    for head in range(heads):
        r.cum[head] = logs[head : head + 1]
        r.col[head] = jnp.broadcast_to(columns[:, head : head + 1], (tokens, LANES))
    for head in range(heads):
        r.decays[x, z, core, head] = jnp.exp(r.col[head, tokens - 1 : tokens, :])

    def local_states(pair):
        lanes = pair_lanes(pair)
        log = jnp.where(first_head, r.col[2 * pair], r.col[2 * pair + 1])
        tail = jnp.exp(log[tokens - 1 :] - log)
        r.tail[:, lanes] = tail
        r.inc[:, lanes] = jnp.exp(log)
        high, low = split(jnp.transpose(r.x[:, lanes].astype(f32) * tail))
        r.state[pl.ds(pl.multiple_of(pair * LANES, LANES), LANES)] = dot(high, r.b[...]) + dot(
            low, r.b[...]
        )

    loop(pairs, local_states)
    pl.semaphore_wait(barrier, count + groups - 2)

    scan_send(r.state, r.got, r.state_sems.at[0], r.state_sems.at[1])
    for step in range(1, NZ):
        peer = ctx_of(x, lax.rem(z + step, NZ), core)
        remote(r.decays.at[x, z, core], r.decays.at[x, z, core], r.decay_sent, r.decay_z.at[step], ctx=peer).start()
    w_home = local(r.w, r.w_all.at[x, z, core], r.w_own)
    w_home.start()
    for step in range(1, NZ):
        peer = ctx_of(x, lax.rem(z + step, NZ), core)
        remote(r.w, r.w_all.at[x, z, core], r.w_sent, r.w_z.at[step], ctx=peer).start()
    for turn in range(NX - 1):
        peer = ctx_of(lax.rem(x + turn + 1, NX), z, core)
        remote(r.w, r.w_all.at[x, z, core], r.w_sent, r.w_x.at[turn], ctx=peer).start()
    right, left = lax.rem(row + 1, groups), lax.rem(row + groups - 1, groups)
    far, near = groups // 2, groups - 1 - groups // 2

    def ring(step):
        for side, most, target, back in ((0, far, right, -step), (1, near, left, step)):
            if step < most:
                piece = lax.rem(row + groups + back, groups)
                if step:
                    wait_for(r.dout_all.at[piece], r.d_came.at[side, step])
                source = r.dout_all.at[piece] if step else r.dout
                remote(
                    source, r.dout_all.at[piece], r.d_sent, r.d_came.at[side, step + 1], head=target
                ).start()

    ring(0)

    scores = dot_nt(r.c[...], r.b[...])
    r.scores[...] = scores
    causal = (
        lax.broadcasted_iota(jnp.int32, (half, half), 0)
        >= lax.broadcasted_iota(jnp.int32, (half, half), 1)
    )

    def inside(pair):
        lanes = pair_lanes(pair)
        parts = []
        for head in (2 * pair, 2 * pair + 1):
            outs = []
            for top in (0, 1):
                high, low = [], []
                at = pl.ds(top * half, half)
                for side in range(top + 1):
                    to = pl.ds(side * half, half)
                    gap = r.col[head, at, :] - r.cum[head, :, to]
                    if side == top:
                        decay = jnp.where(causal, jnp.exp(jnp.where(causal, gap, 0.0)), 0.0)
                    else:
                        decay = jnp.exp(gap)
                    r.decay[head, at, to] = decay
                    h, l = split(decay * r.scores[at, to])
                    r.kern_high[head, at, to] = h
                    r.kern_low[head, at, to] = l
                    high.append(h)
                    low.append(l)
                values = r.x[pl.ds(0, (top + 1) * half), lanes]
                outs.append(
                    dot(jnp.concatenate(high, axis=1), values) + dot(jnp.concatenate(low, axis=1), values)
                )
            parts.append(jnp.concatenate(outs, axis=0))
        r.mixed[:, lanes] = jnp.where(first_head, parts[0], parts[1]) + r.skip[:, lanes] * r.x[
            :, lanes
        ].astype(f32)

    def gate(chunk):
        at = chunk_rows(chunk)
        value = r.z[at, :].astype(f32)
        sigmoid = 1.0 / (1.0 + jnp.exp(-value))
        r.act[at, :] = value * sigmoid
        r.slope[at, :] = sigmoid * (1.0 + value * (1.0 - sigmoid))

    def relay(step):
        source = lax.rem(z + NZ - step, NZ)
        wait_for(r.w_all.at[x, source, core], r.w_z.at[step])
        for turn in range(NX - 1):
            peer = ctx_of(lax.rem(x + turn + 1, NX), z, core)
            piece = r.w_all.at[x, source, core]
            remote(piece, piece, r.w_sent, r.w_x.at[turn], ctx=peer).start()

    loop(pairs // 2, inside)
    spot = x * NC + core
    for step in range(1, NZ):
        wait_for(r.decays.at[x, lax.rem(z + NZ - step, NZ), core], r.decay_z.at[step])
    for step in range(1, NX * NC):
        other = lax.rem(spot + step, NX * NC)
        line = r.decays.at[x, :, core]
        remote(
            line, line, r.decay_sent, r.decay_x.at[step], ctx=ctx_of(other // NC, z, lax.rem(other, NC))
        ).start()
    for step in range(1, NZ):
        relay(step)
        if step % 2 == 0:
            ring(step // 2)
    w_home.wait()
    mine_line = r.w_all.at[x, :, core]
    remote(mine_line, mine_line, r.w_sent, r.w_core.at[0], ctx=twin).start()
    for step in range(1, NX * NC):
        other = lax.rem(spot + NX * NC - step, NX * NC)
        wait_for(r.decays.at[other // NC, :, lax.rem(other, NC)], r.decay_x.at[step])
    scan_turn(
        r.got, r.decays, r.before, r.came_in, r.state_sems.at[2], r.state_sems.at[1], r.state_sems.at[3],
        False,
    )
    for step in range(1, far):
        if step > (NZ - 1) // 2:
            ring(step)
    for turn in range(NX - 1):
        line = r.w_all.at[lax.rem(x + NX - turn - 1, NX), :, core]
        wait_for(line, r.w_x.at[turn])
        remote(line, line, r.w_sent, r.w_core.at[turn + 1], ctx=twin).start()
    lax.fori_loop(pairs // 2, pairs, lambda pair, carry: (inside(pair), carry)[1], 0)
    loop(chunks, gate)
    r.dout_all[row] = r.dout[...]
    wait_for(r.dout_all.at[lax.rem(row + groups - far, groups)], r.d_came.at[0, far])
    if near:
        wait_for(r.dout_all.at[lax.rem(row + near, groups)], r.d_came.at[1, near])

    def turned(piece):
        r.dout_turned[piece] = jnp.transpose(r.dout_all[piece])

    loop(groups, turned)
    for turn in range(NX):
        wait_for(r.w_all.at[lax.rem(x + NX - turn, NX), :, 1 - core], r.w_core.at[turn])
    piece_rows, piece_width = r.w.shape[0], r.dout.shape[1]
    deep = piece_width // (piece_rows * NC)
    line_pieces = NZ // deep

    def project(piece):
        z_from = pl.ds(lax.rem(piece, line_pieces) * deep, deep)
        block = r.w_all[piece // line_pieces, z_from].reshape(piece_width, inner)
        value = dot(r.dout_all[piece], block)

        @pl.when(piece == 0)
        def _():
            r.normed_grad[...] = value

        @pl.when(piece > 0)
        def _():
            r.normed_grad[...] += value

    loop(groups, project)

    wait_for(r.came_in, r.state_sems.at[3])
    in_high, in_low = split(r.came_in[...])
    r.carried[...] = dot_nt(r.c[...], in_high) + dot_nt(r.c[...], in_low)

    def gated_rows(chunk):
        at = chunk_rows(chunk)
        mixed = r.mixed[at, :] + r.carried[at, :] * r.inc[at, :]
        gated = mixed * r.act[at, :]
        r.mixed[at, :] = mixed
        r.gated[at, :] = gated
        square = gated * gated
        product = r.gain[...] * r.normed_grad[at, :] * gated
        fold = lambda value: sum(
            value[:, lane : lane + LANES] for lane in range(LANES, inner, LANES)
        ) + value[:, :LANES]
        r.square[at, :] = fold(square)
        r.product[at, :] = fold(product)

    loop(chunks, gated_rows)
    ones = jnp.ones((8, LANES), f32)
    top_row = lax.broadcasted_iota(jnp.int32, (8, tokens), 0) == 0
    r.sums[...] = jnp.where(
        top_row, dot_nt(ones, r.square[...], HIGH), dot_nt(ones, r.product[...], HIGH)
    )
    others(
        "head", lambda peer: remote(r.sums, r.sums_got.at[row], r.sum_sems.at[0], r.sum_sems.at[1], head=peer).start()
    )
    local(r.sums, r.sums_got.at[row], r.sum_sems.at[1]).start()
    wait_for(r.sums_got, r.sum_sems.at[1])
    total = r.sums_got[0]
    for index in range(1, groups):
        total = total + r.sums_got[index]
    inv = lax.rsqrt(total[0:1] / features + EPSILON)
    pull = inv * inv * inv * (total[1:2] / features)
    both = jnp.transpose(jnp.where(top_row, inv, pull))
    r.inv[...] = jnp.broadcast_to(both[:, 0:1], (tokens, LANES))
    r.pull[...] = jnp.broadcast_to(both[:, 1:2], (tokens, LANES))

    def gradient_rows(chunk, sums):
        at = chunk_rows(chunk)
        wide = lambda value: jnp.concatenate([value] * (inner // LANES), axis=1)
        inv, pull = wide(r.inv[at, :]), wide(r.pull[at, :])
        gated, normed_grad = r.gated[at, :], r.normed_grad[at, :]
        scaled = gated * inv
        r.normed_high[at, :], r.normed_low[at, :] = split(scaled * r.gain[...])
        gated_grad = inv * (r.gain[...] * normed_grad) - gated * pull
        grad = gated_grad * r.act[at, :]
        r.grad_z[at, :] = (gated_grad * r.mixed[at, :] * r.slope[at, :]).astype(bf16)
        r.grad[at, :] = grad
        r.grad_inc[at, :] = grad * r.inc[at, :]
        gain = normed_grad * scaled
        skip = grad * r.x[at, :].astype(f32)
        fold = lambda value: sum(value[at : at + 8] for at in range(8, CHUNK, 8)) + value[:8]
        return sums[0] + fold(gain), sums[1] + fold(skip)

    zero = jnp.zeros((8, inner), f32)
    gain_sum, skip_sum = lax.fori_loop(0, chunks, gradient_rows, (zero, zero))
    gain_sum = jnp.sum(gain_sum, axis=0, keepdims=True)
    skip_sum = jnp.sum(skip_sum, axis=0, keepdims=True)
    for index in range(pairs):
        lanes = slice(index * LANES, (index + 1) * LANES)
        r.small[index : index + 1, :] = gain_sum[:, lanes]
        r.small[pairs + index : pairs + index + 1, :] = skip_sum[:, lanes]

    all_but_one = r.got.at[pl.ds(0, count - 1)]
    wait_for(all_but_one, r.state_sems.at[0])
    wait_for(all_but_one, r.state_sems.at[2])

    def local_gradients(pair):
        lanes = pair_lanes(pair)
        high, low = split(jnp.transpose(r.grad_inc[:, lanes]))
        r.state_grad[pl.ds(pl.multiple_of(pair * LANES, LANES), LANES)] = dot(high, r.c[...]) + dot(
            low, r.c[...]
        )

    loop(pairs, local_gradients)
    scan_send(r.state_grad, r.got_grad, r.back_sems.at[0], r.back_sems.at[1])

    order = [lax.rem(x + step, NX) for step in range(1, NX + 1)]
    depth = NZ // PARTS
    for step in range(NX):
        left_side = jnp.concatenate(
            [r.dout_turned[order[step] * line_pieces + index] for index in range(line_pieces)], axis=0
        )
        value = dot(left_side, r.normed_high[...]) + dot(left_side, r.normed_low[...])
        r.grads[order[step]] = value.reshape(NZ, NC, piece_rows, inner)
        remote(
            r.grads.at[order[step], :, 1 - core], r.twin_got.at[order[step]], r.twin_sems.at[0, step],
            r.twin_sems.at[1, step], ctx=twin,
        ).start()
    others(
        "ctx", lambda peer: remote(r.small, r.small_got.at[mine], r.small_sems.at[0], r.small_sems.at[1], ctx=peer).start()
    )
    local(r.small, r.small_got.at[mine], r.small_sems.at[1]).start()
    for step in range(NX):
        wait_for(r.twin_got.at[order[step]], r.twin_sems.at[1, step])

        def add(index):
            r.mid[order[step], index] = (
                r.grads[order[step], index, core] + r.twin_got[order[step], index]
            )

        loop(NZ, add)
        if step < NX - 1:
            for part in range(PARTS):
                block = pl.ds(part * depth, depth)
                remote(
                    r.mid.at[order[step], block], r.x_got.at[step, block], r.x_sent,
                    r.x_came.at[part, step], ctx=ctx_of(order[step], z, core),
                ).start()

    def products(pair):
        lanes = pair_lanes(pair)
        grad = r.grad[:, lanes]
        high, low = split(grad)
        both = jnp.concatenate([high, low], axis=1)
        values = r.x[:, lanes].astype(f32)
        turned_high, turned_low = split(jnp.transpose(grad))
        outs = []
        for side in (0, 1):
            head = 2 * pair + side
            masked = jnp.where(first_head == (side == 0), values, 0.0).astype(bf16)
            masked = jnp.concatenate([masked, masked], axis=1)
            for top in (0, 1):
                at, to = pl.ds(top * half, half), pl.ds(0, (top + 1) * half)
                value = dot_nt(both[top * half : (top + 1) * half], masked[: (top + 1) * half])
                r.products[at, to] += value * r.decay[head, at, to]
            mine_high = turned_high[side * HDIM : (side + 1) * HDIM]
            mine_low = turned_low[side * HDIM : (side + 1) * HDIM]
            lines = []
            for to in (0, 1):
                at, lane = pl.ds(to * half, tokens - to * half), pl.ds(to * half, half)
                kern = r.kern_high[head, at, lane]
                lines.append(
                    dot(mine_high[:, to * half :], kern)
                    + dot(mine_low[:, to * half :], kern)
                    + dot(mine_high[:, to * half :], r.kern_low[head, at, lane])
                )
            outs.append(jnp.concatenate(lines, axis=1))
        r.grad_values[:, lanes] = jnp.transpose(jnp.concatenate(outs, axis=0)) + r.skip[:, lanes] * grad

    r.products[...] = jnp.zeros_like(r.products)
    loop(pairs, products)
    high, low = split(r.products[...])
    in_high, in_low = split(r.came_in[...])
    out_high, out_low = split(r.grad_inc[...])
    r.part_c[...] = (
        dot(high, r.b[...]) + dot(low, r.b[...])
        + dot(out_high, in_high) + dot(out_low, in_high) + dot(out_high, in_low)
    )
    shared_send(r.part_c, r.got_c, r.c_sems)
    high, low = split(jnp.transpose(r.products[...]))
    r.part_b[...] = dot(high, r.c[...]) + dot(low, r.c[...])

    scan_turn(
        r.got_grad, r.decays, r.before_grad, r.grad_in, r.back_sems.at[2], r.back_sems.at[1],
        r.back_sems.at[3], True,
    )
    shared_turn(r.got_c, r.sum_c, r.grad_c, r.c_sems)

    def fold_part(part):
        block = pl.ds(part * depth, depth)
        for step in range(NX - 1):
            wait_for(r.x_got.at[step, block], r.x_came.at[part, step])

        def fold(turn):
            index = lax.rem(z + turn + 1, NZ)

            @pl.when((index >= part * depth) & (index < (part + 1) * depth))
            def _():
                value = r.mid[x, index]
                for step in range(NX - 1):
                    value = value + r.x_got[step, index]
                r.low[index] = value

                @pl.when(index != z)
                def _():
                    remote(
                        r.low.at[index], r.z_got.at[z], r.z_sent, r.z_came, ctx=ctx_of(x, index, core)
                    ).start()

        loop(NZ, fold)

    fold_part(0)
    wait_for(r.grad_in, r.back_sems.at[3])
    in_high, in_low = split(r.grad_in[...])
    r.carried[...] = dot_nt(r.b[...], in_high) + dot_nt(r.b[...], in_low)

    def weigh(chunk):
        at = chunk_rows(chunk)
        tail = r.tail[at, :]
        r.grad_x[at, :] = (r.grad_values[at, :] + r.carried[at, :] * tail).astype(bf16)
        r.grad_inc[at, :] = r.x[at, :].astype(f32) * tail

    loop(chunks, weigh)
    out_high, out_low = split(r.grad_inc[...])
    r.part_b[...] += dot(out_high, in_high) + dot(out_low, in_high) + dot(out_high, in_low)
    shared_send(r.part_b, r.got_b, r.b_sems)
    for part in range(1, PARTS):
        fold_part(part)
    local(r.low.at[z], r.z_got.at[z], r.z_came).start()
    shared_turn(r.got_b, r.sum_b, r.grad_b, r.b_sems)
    wait_for(r.small_got, r.small_sems.at[1])
    r.small_total[...] = lax.fori_loop(
        1, count, lambda index, value: value + r.small_got[index], r.small_got[0]
    )
    wait_for(r.z_got, r.z_came)
    value = r.z_got[0]
    for index in range(1, NZ):
        value = value + r.z_got[index]
    r.grad_w[...] = value

    shared_end(r.got_c, r.grad_c, r.c_sems)
    shared_end(r.got_b, r.grad_b, r.b_sems)
    wait_for(all_but_one, r.back_sems.at[0])
    wait_for(all_but_one, r.back_sems.at[2])
    wait_for(r.small_got.at[pl.ds(0, count - 1)], r.small_sems.at[0])
    for step in range(NX):
        wait_for(r.twin_got.at[step], r.twin_sems.at[0, step])
    for step in range(NX - 1):
        wait_for(r.x_got.at[step], r.x_sent)
    wait_for(r.z_got.at[pl.ds(0, NZ - 1)], r.z_sent)
    wait_for(r.dout_all.at[pl.ds(0, groups - 1)], r.d_sent)
    wait_for(r.sums_got.at[pl.ds(0, groups - 1)], r.sum_sems.at[0])
    wait_for(r.decays.at[0, pl.ds(0, NZ - 1), 0], r.decay_sent)
    for step in range(1, NX * NC):
        wait_for(r.decays.at[0, :, 0], r.decay_sent)
    for turn in range(2 * NX - 1):
        wait_for(r.w_all.at[turn % NX, :, 0], r.w_sent)
    wait_for(r.w_all.at[0, pl.ds(0, NZ - 1), 0], r.w_sent)


def per_device(xin, zin, bmat, cmat, ldec, dskip, gain, w_out, dout):
    shape = jax.ShapeDtypeStruct
    dma = pltpu.SemaphoreType.DMA
    blocks, groups = lax.axis_size("ctx"), lax.axis_size("head")
    heads, tokens = ldec.shape
    inner, width = heads * HDIM, bmat.shape[1]
    rows, share = inner // blocks, tokens // groups
    piece = w_out.shape
    wide = pltpu.VMEM((tokens, inner), f32)
    wide_half = pltpu.VMEM((tokens, inner), bf16)
    narrow = pltpu.VMEM((tokens, LANES), f32)
    square = (heads, tokens, tokens)
    slices = pltpu.VMEM((blocks, rows, width), f32)
    flat = pltpu.VMEM((inner, width), f32)
    operands = {
        "x": xin, "z": zin, "b": bmat, "c": cmat, "ldec": ldec,
        "skip": jnp.repeat(dskip, HDIM)[None], "gain": gain[None], "w": w_out, "dout": dout,
    }
    outs = {
        "grad_x": shape((tokens, inner), bf16),
        "grad_z": shape((tokens, inner), bf16),
        "grad_b": shape((tokens, width), f32),
        "grad_c": shape((tokens, width), f32),
        "grad_w": shape(piece, f32),
        "small_total": shape((8, LANES), f32),
    }
    scratch = {
        "cum": pltpu.VMEM((heads, 1, tokens), f32), "col": pltpu.VMEM((heads, tokens, LANES), f32),
        "tail": wide, "inc": wide, "scores": pltpu.VMEM((tokens, tokens), f32),
        "decay": pltpu.VMEM(square, f32), "kern_high": pltpu.VMEM(square, bf16),
        "kern_low": pltpu.VMEM(square, bf16), "mixed": wide, "act": wide, "slope": wide, "gated": wide,
        "normed_grad": wide, "carried": wide, "grad": wide, "grad_inc": wide, "grad_values": wide,
        "normed_high": wide_half, "normed_low": wide_half, "square": narrow, "product": narrow,
        "inv": narrow, "pull": narrow, "products": pltpu.VMEM((tokens, tokens), f32),
        "part_b": narrow, "part_c": narrow,
        "state": flat, "state_grad": flat, "came_in": flat, "grad_in": flat,
        "got": slices, "before": slices, "got_grad": slices, "before_grad": slices,
        "state_sems": dma((4,)), "back_sems": dma((4,)),
        "decays": pltpu.VMEM((NX, NZ, NC, heads, 1, LANES), f32), "decay_sent": dma(()), "decay_z": dma((NZ,)),
        "decay_x": dma((NX * NC,)),
        "w_all": pltpu.VMEM((NX, NZ, NC) + piece, bf16), "w_sent": dma(()), "w_z": dma((NZ,)),
        "w_x": dma((NX,)), "w_core": dma((NX,)), "w_own": dma(()),
        "dout_all": pltpu.VMEM((groups,) + dout.shape, bf16), "d_sent": dma(()),
        "d_came": dma((2, groups // 2 + 1)),
        "dout_turned": pltpu.VMEM((groups, dout.shape[1], tokens), bf16),
        "sums": pltpu.VMEM((8, tokens), f32), "sums_got": pltpu.VMEM((groups, 8, tokens), f32),
        "sum_sems": dma((2,)),
        "small": pltpu.VMEM((8, LANES), f32), "small_got": pltpu.VMEM((blocks, 8, LANES), f32),
        "small_sems": dma((2,)),
        "grads": pltpu.VMEM((NX, NZ, NC) + piece, f32), "twin_got": pltpu.VMEM((NX, NZ) + piece, f32),
        "mid": pltpu.VMEM((NX, NZ) + piece, f32), "x_got": pltpu.VMEM((NX - 1, NZ) + piece, f32),
        "low": pltpu.VMEM((NZ,) + piece, f32), "z_got": pltpu.VMEM((NZ,) + piece, f32),
        "twin_sems": dma((2, NX)), "x_sent": dma(()), "x_came": dma((PARTS, NX)), "z_sent": dma(()),
        "z_came": dma(()),
        "got_b": pltpu.VMEM((groups, share, width), f32), "sum_b": pltpu.VMEM((share, width), f32),
        "b_sems": dma((4,)),
        "got_c": pltpu.VMEM((groups, share, width), f32), "sum_c": pltpu.VMEM((share, width), f32),
        "c_sems": dma((4,)),
    }
    names = tuple(operands) + tuple(outs) + tuple(scratch)
    vmem = pl.BlockSpec(memory_space=pltpu.VMEM)
    grad_x, grad_z, grad_b, grad_c, grad_w, small = pl.pallas_call(
        lambda *refs: whole_kernel(names, *refs),
        out_shape=tuple(outs.values()),
        in_specs=[vmem] * len(operands),
        out_specs=(vmem,) * len(outs),
        scratch_shapes=list(scratch.values()),
        name="whole",
        compiler_params=pltpu.CompilerParams(
            collective_id=0, has_side_effects=True, vmem_limit_bytes=VMEM_LIMIT
        ),
    )(*operands.values())
    pairs = heads // 2
    grad_gain = small[:pairs].reshape(-1)
    grad_skip = jnp.sum(small[pairs : 2 * pairs].reshape(heads, HDIM), axis=1)
    return grad_x, grad_z, grad_b, grad_c, grad_w, grad_gain, grad_skip


def solution(mesh):
    return jax.shard_map(
        per_device,
        mesh=mesh,
        in_specs=(
            P("ctx", "head"), P("ctx", "head"), P("ctx", None), P("ctx", None), P("head", "ctx"),
            P("head"), P("head"), P("ctx", "head"), P("ctx", "head"),
        ),
        out_specs=(
            P("ctx", "head"), P("ctx", "head"), P("ctx", None), P("ctx", None), P("ctx", "head"),
            P("head"), P("head"),
        ),
        check_vma=False,
    )
```

```python
import types
import jax
import jax.numpy as jnp
from jax import lax
from jax.experimental import pallas as pl
from jax.experimental.pallas import tpu as pltpu
from jax.sharding import PartitionSpec as P

HDIM = 64
HIGH = lax.Precision.HIGHEST
EPSILON = 1e-05
MESH = pl.DeviceIdType.MESH
NX, NZ, NC = 4, 8, 2
PARTS = 4
LANES = 128
CHUNK = 16
VMEM_LIMIT = 56 * 2**20
f32, bf16 = jnp.float32, jnp.bfloat16


def remote(src, dst, sent, came, **where):
    return pltpu.make_async_remote_copy(
        src_ref=src, dst_ref=dst, send_sem=sent, recv_sem=came, device_id=where, device_id_type=MESH
    )


def local(src, dst, sem):
    return pltpu.make_async_copy(src, dst, sem)


def wait_for(ref, sem):
    local(ref, ref, sem).wait()


def others(axis, act):
    count, mine = lax.axis_size(axis), lax.axis_index(axis)

    def turn(step, carry):
        act(lax.rem(mine + step, count))
        return carry

    lax.fori_loop(1, count, turn, 0)


def ctx_of(x, z, core):
    return (x * NZ + z) * NC + core


def split(value):
    high = value.astype(bf16)
    return high, (value - high.astype(f32)).astype(bf16)


def dot(a, b):
    return jnp.dot(a, b, preferred_element_type=f32)


def dot_nt(a, b, precision=None):
    return lax.dot_general(
        a, b, (((1,), (1,)), ((), ())), preferred_element_type=f32, precision=precision
    )


def rows_at(ref, index, rows):
    return ref.at[pl.ds(pl.multiple_of(index * rows, rows), rows)]


def loop(count, body):
    def turn(index, carry):
        body(index)
        return carry

    lax.fori_loop(0, count, turn, 0)


def chip_peers(act):
    mine = lax.axis_index("ctx")
    chips = NX * NZ

    def turn(step, carry):
        act(lax.rem(mine // NC + step, chips))
        return carry

    lax.fori_loop(1, chips, turn, 0)


def joined(own, other, is_first):
    return jnp.where(is_first, own, other), jnp.where(is_first, other, own)


class Scan:
    def __init__(self, r, name, backward):
        self.state, self.came = getattr(r, name + "_state"), getattr(r, name + "_came")
        self.twin, self.half = getattr(r, name + "_twin"), getattr(r, name + "_half")
        self.got, self.before = getattr(r, name + "_got"), getattr(r, name + "_before")
        self.entry, self.give = getattr(r, name + "_entry"), getattr(r, name + "_give")
        self.sems, self.r, self.backward = getattr(r, name + "_sems"), r, backward
        mine = lax.axis_index("ctx")
        self.core, self.chip = lax.rem(mine, NC), mine // NC
        self.first = NC - 1 if backward else 0
        self.is_first = self.core == self.first
        self.heads = self.half.shape[0] // HDIM

    def to_twin(self):
        rows = self.half.shape[0]
        remote(
            rows_at(self.state, 1 - self.core, rows), self.twin, self.sems.at[0], self.sems.at[1],
            ctx=self.chip * NC + 1 - self.core,
        ).start()

    def send(self):
        wait_for(self.twin, self.sems.at[1])
        for index in range(self.heads):
            at = pl.ds(index * HDIM, HDIM)
            from_state = pl.ds(pl.multiple_of(self.core * self.half.shape[0] + index * HDIM, HDIM), HDIM)
            first, second = joined(self.state[from_state], self.twin[at], self.is_first)
            factor = self.r.pair_decays[1 - self.first, self.core * self.heads + index]
            self.half[at] = factor * first + second
        rows = self.got.shape[1]
        chip_peers(
            lambda peer: remote(
                rows_at(self.half, peer, rows), self.got.at[self.chip], self.sems.at[2], self.sems.at[3],
                ctx=peer * NC + self.core,
            ).start()
        )
        local(rows_at(self.half, self.chip, rows), self.got.at[self.chip], self.sems.at[3]).start()

    def turn(self):
        chips, rows = self.got.shape[0], self.got.shape[1]
        head = self.chip // (HDIM // rows)
        wait_for(self.got, self.sems.at[3])

        def step(index, total):
            index = chips - 1 - index if self.backward else index
            self.before[index] = total
            return self.r.decays[index // NZ, lax.rem(index, NZ), head] * total + self.got[index]

        lax.fori_loop(0, chips, step, jnp.zeros(self.got.shape[1:], f32), unroll=4)
        home = rows_at(self.entry, self.chip, rows)
        chip_peers(
            lambda peer: remote(
                self.before.at[peer], home, self.sems.at[4], self.sems.at[5], ctx=peer * NC + self.core
            ).start()
        )
        local(self.before.at[self.chip], home, self.sems.at[5]).start()

    def share(self):
        wait_for(self.entry, self.sems.at[5])
        rows = self.half.shape[0]
        for index in range(self.heads):
            at = pl.ds(index * HDIM, HDIM)
            to = pl.ds(pl.multiple_of(self.core * rows + index * HDIM, HDIM), HDIM)
            entry = self.entry[at]
            first, _ = joined(self.state[to], self.twin[at], self.is_first)
            factor = self.r.pair_decays[self.first, self.core * self.heads + index]
            later = factor * entry + first
            self.came[to] = jnp.where(self.is_first, entry, later)
            self.give[at] = jnp.where(self.is_first, later, entry)
        remote(
            self.give, rows_at(self.came, self.core, rows), self.sems.at[6], self.sems.at[7],
            ctx=self.chip * NC + 1 - self.core,
        ).start()

    def finish(self):
        wait_for(self.give, self.sems.at[7])

    def drain(self):
        most = self.got.at[pl.ds(0, self.got.shape[0] - 1)]
        wait_for(self.twin, self.sems.at[0])
        wait_for(most, self.sems.at[2])
        wait_for(most, self.sems.at[4])
        wait_for(self.give, self.sems.at[6])


def shared_send(part, got, sems):
    mine, rows = lax.axis_index("head"), got.shape[1]
    others(
        "head",
        lambda peer: remote(rows_at(part, peer, rows), got.at[mine], sems.at[0], sems.at[1], head=peer).start(),
    )
    local(rows_at(part, mine, rows), got.at[mine], sems.at[1]).start()


def shared_turn(got, summed, total, sems):
    mine, rows = lax.axis_index("head"), got.shape[1]
    wait_for(got, sems.at[1])
    value = got[0]
    for index in range(1, got.shape[0]):
        value = value + got[index]
    summed[...] = value
    home = rows_at(total, mine, rows)
    others("head", lambda peer: remote(summed, home, sems.at[2], sems.at[3], head=peer).start())
    local(summed, home, sems.at[3]).start()


def shared_end(got, total, sems):
    peers = got.at[pl.ds(0, got.shape[0] - 1)]
    wait_for(total, sems.at[3])
    wait_for(peers, sems.at[0])
    wait_for(peers, sems.at[2])


def whole_kernel(names, *refs):
    r = types.SimpleNamespace(**dict(zip(names, refs)))
    mine, row = lax.axis_index("ctx"), lax.axis_index("head")
    groups = lax.axis_size("head")
    x, z, core = mine // (NZ * NC), lax.rem(mine // NC, NZ), lax.rem(mine, NC)
    twin = ctx_of(x, z, 1 - core)
    heads, tokens = r.ldec.shape
    pairs = heads // 2
    inner = heads * HDIM
    half = tokens // 2
    features = inner * groups
    chunks = tokens // CHUNK
    first_head = lax.broadcasted_iota(jnp.int32, (tokens, LANES), 1) < HDIM

    def pair_lanes(pair):
        return pl.ds(pl.multiple_of(pair * LANES, LANES), LANES)

    def chunk_rows(chunk):
        return pl.ds(pl.multiple_of(chunk * CHUNK, CHUNK), CHUNK)

    barrier = pltpu.get_barrier_semaphore()

    def greet(**where):
        pl.semaphore_signal(barrier, inc=1, device_id=where, device_id_type=MESH)

    greet(ctx=twin)
    chip_peers(lambda peer: greet(ctx=peer * NC + core))
    others("head", lambda peer: greet(head=peer))

    r.gain[...] = r.gain_in[...].reshape(1, inner)
    for pair in range(pairs):
        r.skip[:, pair * LANES : (pair + 1) * LANES] = jnp.where(
            first_head[:1], r.dskip[2 * pair], r.dskip[2 * pair + 1]
        )
    token_of = lax.broadcasted_iota(jnp.int32, (tokens, tokens), 0)
    other_of = lax.broadcasted_iota(jnp.int32, (tokens, tokens), 1)
    logs = dot_nt(r.ldec[...], (token_of >= other_of).astype(f32), HIGH)
    columns = jnp.transpose(logs)
    for head in range(heads):
        r.cum[head] = logs[head : head + 1]
        r.col[head] = jnp.broadcast_to(columns[:, head : head + 1], (tokens, LANES))
    for head in range(heads):
        r.pair_decays[core, head] = jnp.exp(r.col[head, tokens - 1 : tokens, :])

    def local_states(pair):
        lanes = pair_lanes(pair)
        log = jnp.where(first_head, r.col[2 * pair], r.col[2 * pair + 1])
        tail = jnp.exp(log[tokens - 1 :] - log)
        r.tail[:, lanes] = tail
        r.inc[:, lanes] = jnp.exp(log)
        high, low = split(jnp.transpose(r.x[:, lanes].astype(f32) * tail))
        r.fore_state[pl.ds(pl.multiple_of(pair * LANES, LANES), LANES)] = dot(high, r.b[...]) + dot(
            low, r.b[...]
        )

    loop(pairs, local_states)
    pl.semaphore_wait(barrier, NX * NZ + groups - 1)

    fore, back = Scan(r, "fore", False), Scan(r, "back", True)
    fore.to_twin()
    mine_decays = r.pair_decays.at[core]
    remote(mine_decays, mine_decays, r.pair_sems.at[0], r.pair_sems.at[1], ctx=twin).start()
    w_home = local(r.w, r.w_all.at[x, z, core], r.w_own)
    w_home.start()
    for step in range(1, NZ):
        peer = ctx_of(x, lax.rem(z + step, NZ), core)
        remote(r.w, r.w_all.at[x, z, core], r.w_sent, r.w_z.at[step], ctx=peer).start()
    for turn in range(NX - 1):
        peer = ctx_of(lax.rem(x + turn + 1, NX), z, core)
        remote(r.w, r.w_all.at[x, z, core], r.w_sent, r.w_x.at[turn], ctx=peer).start()
    right, left = lax.rem(row + 1, groups), lax.rem(row + groups - 1, groups)
    far, near = groups // 2, groups - 1 - groups // 2

    def ring(step):
        for side, most, target, back in ((0, far, right, -step), (1, near, left, step)):
            if step < most:
                piece = lax.rem(row + groups + back, groups)
                if step:
                    wait_for(r.dout_all.at[piece], r.d_came.at[side, step])
                source = r.dout_all.at[piece] if step else r.dout
                remote(
                    source, r.dout_all.at[piece], r.d_sent, r.d_came.at[side, step + 1], head=target
                ).start()

    ring(0)

    scores = dot_nt(r.c[...], r.b[...])
    r.scores[...] = scores
    causal = (
        lax.broadcasted_iota(jnp.int32, (half, half), 0)
        >= lax.broadcasted_iota(jnp.int32, (half, half), 1)
    )

    def inside(pair):
        lanes = pair_lanes(pair)
        parts = []
        for head in (2 * pair, 2 * pair + 1):
            outs = []
            for top in (0, 1):
                high, low = [], []
                at = pl.ds(top * half, half)
                for side in range(top + 1):
                    to = pl.ds(side * half, half)
                    gap = r.col[head, at, :] - r.cum[head, :, to]
                    if side == top:
                        decay = jnp.where(causal, jnp.exp(jnp.where(causal, gap, 0.0)), 0.0)
                    else:
                        decay = jnp.exp(gap)
                    r.decay[head, at, to] = decay
                    h, l = split(decay * r.scores[at, to])
                    r.kern_high[head, at, to] = h
                    r.kern_low[head, at, to] = l
                    high.append(h)
                    low.append(l)
                values = r.x[pl.ds(0, (top + 1) * half), lanes]
                outs.append(
                    dot(jnp.concatenate(high, axis=1), values) + dot(jnp.concatenate(low, axis=1), values)
                )
            parts.append(jnp.concatenate(outs, axis=0))
        r.mixed[:, lanes] = jnp.where(first_head, parts[0], parts[1]) + r.skip[:, lanes] * r.x[
            :, lanes
        ].astype(f32)

    def gate(chunk):
        at = chunk_rows(chunk)
        value = r.z[at, :].astype(f32)
        sigmoid = 1.0 / (1.0 + jnp.exp(-value))
        r.act[at, :] = value * sigmoid
        r.slope[at, :] = sigmoid * (1.0 + value * (1.0 - sigmoid))

    def relay(step):
        source = lax.rem(z + NZ - step, NZ)
        wait_for(r.w_all.at[x, source, core], r.w_z.at[step])
        for turn in range(NX - 1):
            peer = ctx_of(lax.rem(x + turn + 1, NX), z, core)
            piece = r.w_all.at[x, source, core]
            remote(piece, piece, r.w_sent, r.w_x.at[turn], ctx=peer).start()

    wait_for(r.pair_decays.at[1 - core], r.pair_sems.at[1])
    for index in range(heads // NC):
        head = core * (heads // NC) + index
        r.decays[x, z, index] = r.pair_decays[0, head] * r.pair_decays[1, head]
    for step in range(1, NZ):
        peer = ctx_of(x, lax.rem(z + step, NZ), core)
        remote(r.decays.at[x, z], r.decays.at[x, z], r.decay_sent, r.decay_z.at[step], ctx=peer).start()
    fore.send()
    loop(pairs // 2, inside)
    if far > 1:
        ring(1)
    for step in range(1, NZ):
        relay(step)
    if far > 2:
        ring(2)
    w_home.wait()
    mine_line = r.w_all.at[x, :, core]
    remote(mine_line, mine_line, r.w_sent, r.w_core.at[0], ctx=twin).start()
    for step in range(1, NZ):
        wait_for(r.decays.at[x, lax.rem(z + NZ - step, NZ)], r.decay_z.at[step])
    for step in range(1, NX):
        line = r.decays.at[x]
        remote(line, line, r.decay_sent, r.decay_x.at[step], ctx=ctx_of(lax.rem(x + step, NX), z, core)).start()
    for step in range(1, NX):
        wait_for(r.decays.at[lax.rem(x + NX - step, NX)], r.decay_x.at[step])
    fore.turn()
    lax.fori_loop(pairs // 2, pairs, lambda pair, carry: (inside(pair), carry)[1], 0)
    for step in range(3, far):
        ring(step)
    loop(chunks, gate)
    for turn in range(NX - 1):
        line = r.w_all.at[lax.rem(x + NX - turn - 1, NX), :, core]
        wait_for(line, r.w_x.at[turn])
        remote(line, line, r.w_sent, r.w_core.at[turn + 1], ctx=twin).start()
    r.dout_all[row] = r.dout[...]
    wait_for(r.dout_all.at[lax.rem(row + groups - far, groups)], r.d_came.at[0, far])
    if near:
        wait_for(r.dout_all.at[lax.rem(row + near, groups)], r.d_came.at[1, near])

    def turned(piece):
        r.dout_turned[piece] = jnp.transpose(r.dout_all[piece])

    loop(groups, turned)
    piece_rows, piece_width = r.w.shape[0], r.dout.shape[1]
    line_pieces = NZ * NC * piece_rows // piece_width

    for turn in range(NX):
        wait_for(r.w_all.at[lax.rem(x + NX - turn, NX), :, 1 - core], r.w_core.at[turn])
    r.normed_grad[...] = dot(
        jnp.concatenate([r.dout_all[piece] for piece in range(groups)], axis=1),
        r.w_all[...].reshape(groups * piece_width, inner),
    )

    fore.share()
    fore.finish()
    in_high, in_low = split(r.fore_came[...])
    r.carried[...] = dot_nt(r.c[...], in_high) + dot_nt(r.c[...], in_low)

    def gated_rows(chunk):
        at = chunk_rows(chunk)
        mixed = r.mixed[at, :] + r.carried[at, :] * r.inc[at, :]
        gated = mixed * r.act[at, :]
        r.mixed[at, :] = mixed
        r.gated[at, :] = gated
        r.square[at, :] = lane_fold(gated * gated)
        r.product[at, :] = lane_fold(r.gain[...] * r.normed_grad[at, :] * gated)

    def lane_fold(value):
        return sum(value[:, lane : lane + LANES] for lane in range(LANES, inner, LANES)) + value[:, :LANES]

    ones = jnp.ones((8, LANES), f32)

    def wide(value):
        return jnp.concatenate([value] * (inner // LANES), axis=1)

    loop(chunks, gated_rows)
    top_row = lax.broadcasted_iota(jnp.int32, (8, tokens), 0) == 0
    r.sums[...] = jnp.where(
        top_row, dot_nt(ones, r.square[...], HIGH), dot_nt(ones, r.product[...], HIGH)
    )
    others(
        "head",
        lambda peer: remote(r.sums, r.sums_got.at[row], r.sum_sems.at[0], r.sum_sems.at[1], head=peer).start(),
    )
    local(r.sums, r.sums_got.at[row], r.sum_sems.at[1]).start()
    wait_for(r.sums_got, r.sum_sems.at[1])
    total = r.sums_got[0]
    for index in range(1, groups):
        total = total + r.sums_got[index]
    total = total / features
    inv = lax.rsqrt(total[0:1] + EPSILON)
    pull = inv * inv * inv * total[1:2]
    both = jnp.transpose(jnp.where(top_row, inv, pull))
    r.inv[...] = jnp.broadcast_to(both[:, 0:1], (tokens, LANES))
    r.pull[...] = jnp.broadcast_to(both[:, 1:2], (tokens, LANES))

    def gradient_rows(chunk, sums):
        at = chunk_rows(chunk)
        inv, pull = wide(r.inv[at, :]), wide(r.pull[at, :])
        gated, normed_grad = r.gated[at, :], r.normed_grad[at, :]
        scaled = gated * inv
        r.normed_high[at, :], r.normed_low[at, :] = split(scaled * r.gain[...])
        gated_grad = inv * (r.gain[...] * normed_grad) - gated * pull
        grad = gated_grad * r.act[at, :]
        r.grad_z[at, :] = (gated_grad * r.mixed[at, :] * r.slope[at, :]).astype(bf16)
        r.grad[at, :] = grad
        r.grad_inc[at, :] = grad * r.inc[at, :]
        gain = normed_grad * scaled
        skip = grad * r.x[at, :].astype(f32)
        fold = lambda value: sum(value[at : at + 8] for at in range(8, CHUNK, 8)) + value[:8]
        return sums[0] + fold(gain), sums[1] + fold(skip)

    zero = jnp.zeros((8, inner), f32)
    gain_sum, skip_sum = lax.fori_loop(0, chunks, gradient_rows, (zero, zero))
    gain_sum = jnp.sum(gain_sum, axis=0, keepdims=True)
    skip_sum = jnp.sum(skip_sum, axis=0, keepdims=True)
    for index in range(pairs):
        lanes = slice(index * LANES, (index + 1) * LANES)
        r.small[index : index + 1, :] = gain_sum[:, lanes]
        r.small[pairs + index : pairs + index + 1, :] = skip_sum[:, lanes]

    def local_gradients(pair):
        lanes = pair_lanes(pair)
        high, low = split(jnp.transpose(r.grad_inc[:, lanes]))
        r.back_state[pl.ds(pl.multiple_of(pair * LANES, LANES), LANES)] = dot(high, r.c[...]) + dot(
            low, r.c[...]
        )

    loop(pairs, local_gradients)
    back.to_twin()

    order = [lax.rem(x + step, NX) for step in range(1, NX + 1)]
    depth = NZ // PARTS
    for step in range(NX):
        left_side = jnp.concatenate(
            [r.dout_turned[order[step] * line_pieces + index] for index in range(line_pieces)], axis=0
        )
        value = dot(left_side, r.normed_high[...]) + dot(left_side, r.normed_low[...])
        r.grads[order[step]] = value.reshape(NZ, NC, piece_rows, inner)
        remote(
            r.grads.at[order[step], :, 1 - core], r.twin_got.at[order[step]], r.twin_sems.at[0, step],
            r.twin_sems.at[1, step], ctx=twin,
        ).start()

    remote(r.small, r.small_twin, r.small_sems.at[0], r.small_sems.at[1], ctx=twin).start()
    back.send()
    wait_for(r.small_twin, r.small_sems.at[1])
    r.small_z[z] = r.small[...] + r.small_twin[...]
    for step in range(1, NZ):
        peer = ctx_of(x, lax.rem(z + step, NZ), core)
        remote(r.small_z.at[z], r.small_z.at[z], r.small_sems.at[2], r.small_sems.at[3], ctx=peer).start()
    def products(pair):
        lanes = pair_lanes(pair)
        grad = r.grad[:, lanes]
        high, low = split(grad)
        both = jnp.concatenate([high, low], axis=1)
        values = r.x[:, lanes].astype(f32)
        turned_high, turned_low = split(jnp.transpose(grad))
        outs = []
        for side in (0, 1):
            head = 2 * pair + side
            masked = jnp.where(first_head == (side == 0), values, 0.0).astype(bf16)
            masked = jnp.concatenate([masked, masked], axis=1)
            for top in (0, 1):
                at, to = pl.ds(top * half, half), pl.ds(0, (top + 1) * half)
                value = dot_nt(both[top * half : (top + 1) * half], masked[: (top + 1) * half])
                r.products[at, to] += value * r.decay[head, at, to]
            mine_high = turned_high[side * HDIM : (side + 1) * HDIM]
            mine_low = turned_low[side * HDIM : (side + 1) * HDIM]
            lines = []
            for to in (0, 1):
                at, lane = pl.ds(to * half, tokens - to * half), pl.ds(to * half, half)
                kern = r.kern_high[head, at, lane]
                lines.append(
                    dot(mine_high[:, to * half :], kern)
                    + dot(mine_low[:, to * half :], kern)
                    + dot(mine_high[:, to * half :], r.kern_low[head, at, lane])
                )
            outs.append(jnp.concatenate(lines, axis=1))
        r.grad_values[:, lanes] = jnp.transpose(jnp.concatenate(outs, axis=0)) + r.skip[:, lanes] * grad

    r.products[...] = jnp.zeros_like(r.products)
    loop(pairs, products)
    for step in range(NX):
        wait_for(r.twin_got.at[order[step]], r.twin_sems.at[1, step])

        def add(index):
            r.mid[order[step], index] = (
                r.grads[order[step], index, core] + r.twin_got[order[step], index]
            )

        loop(NZ, add)

    def along_x(part):
        for step in range(NX - 1):
            block = pl.ds(part * depth, depth)
            remote(
                r.mid.at[order[step], block], r.x_got.at[step, block], r.x_sent,
                r.x_came.at[part, step], ctx=ctx_of(order[step], z, core),
            ).start()

    along_x(0)
    high, low = split(r.products[...])
    in_high, in_low = split(r.fore_came[...])
    out_high, out_low = split(r.grad_inc[...])
    r.part_c[...] = (
        dot(high, r.b[...]) + dot(low, r.b[...])
        + dot(out_high, in_high) + dot(out_low, in_high) + dot(out_high, in_low)
    )
    shared_send(r.part_c, r.got_c, r.c_sems)
    high, low = split(jnp.transpose(r.products[...]))
    r.part_b[...] = dot(high, r.c[...]) + dot(low, r.c[...])

    def fold_part(part):
        block = pl.ds(part * depth, depth)
        for step in range(NX - 1):
            wait_for(r.x_got.at[step, block], r.x_came.at[part, step])

        def fold(turn):
            index = lax.rem(z + turn + 1, NZ)

            @pl.when((index >= part * depth) & (index < (part + 1) * depth))
            def _():
                value = r.mid[x, index]
                for step in range(NX - 1):
                    value = value + r.x_got[step, index]
                r.low[index] = value

                @pl.when(index != z)
                def _():
                    remote(
                        r.low.at[index], r.z_got.at[z], r.z_sent, r.z_came, ctx=ctx_of(x, index, core)
                    ).start()

        loop(NZ, fold)

    back.turn()
    for part in range(1, PARTS):
        along_x(part)
    shared_turn(r.got_c, r.sum_c, r.grad_c, r.c_sems)

    fold_part(0)
    back.share()
    wait_for(r.small_z.at[pl.ds(0, NZ - 1)], r.small_sems.at[3])
    value = r.small_z[0]
    for index in range(1, NZ):
        value = value + r.small_z[index]
    r.small_x[x] = value
    for step in range(1, NX):
        peer = ctx_of(lax.rem(x + step, NX), z, core)
        remote(r.small_x.at[x], r.small_x.at[x], r.small_sems.at[4], r.small_sems.at[5], ctx=peer).start()
    back.finish()
    in_high, in_low = split(r.back_came[...])
    r.carried[...] = dot_nt(r.b[...], in_high) + dot_nt(r.b[...], in_low)

    def weigh(chunk):
        at = chunk_rows(chunk)
        tail = r.tail[at, :]
        r.grad_x[at, :] = (r.grad_values[at, :] + r.carried[at, :] * tail).astype(bf16)
        r.grad_inc[at, :] = r.x[at, :].astype(f32) * tail

    loop(chunks, weigh)
    out_high, out_low = split(r.grad_inc[...])
    r.part_b[...] += dot(out_high, in_high) + dot(out_low, in_high) + dot(out_high, in_low)
    shared_send(r.part_b, r.got_b, r.b_sems)
    for part in range(1, PARTS):
        fold_part(part)
        if part == PARTS // 2:
            shared_turn(r.got_b, r.sum_b, r.grad_b, r.b_sems)
    local(r.low.at[z], r.z_got.at[z], r.z_came).start()
    wait_for(r.small_x.at[pl.ds(0, NX - 1)], r.small_sems.at[5])
    value = r.small_x[0]
    for index in range(1, NX):
        value = value + r.small_x[index]
    r.small_total[...] = value
    wait_for(r.z_got, r.z_came)
    value = r.z_got[0]
    for index in range(1, NZ):
        value = value + r.z_got[index]
    r.grad_w[...] = value

    shared_end(r.got_c, r.grad_c, r.c_sems)
    shared_end(r.got_b, r.grad_b, r.b_sems)
    fore.drain()
    back.drain()
    wait_for(r.pair_decays.at[core], r.pair_sems.at[0])
    wait_for(r.small, r.small_sems.at[0])
    wait_for(r.small_z.at[pl.ds(0, NZ - 1)], r.small_sems.at[2])
    wait_for(r.small_x.at[pl.ds(0, NX - 1)], r.small_sems.at[4])
    for step in range(NX):
        wait_for(r.twin_got.at[step], r.twin_sems.at[0, step])
    for step in range(NX - 1):
        wait_for(r.x_got.at[step], r.x_sent)
    wait_for(r.z_got.at[pl.ds(0, NZ - 1)], r.z_sent)
    wait_for(r.dout_all.at[pl.ds(0, groups - 1)], r.d_sent)
    wait_for(r.sums_got.at[pl.ds(0, groups - 1)], r.sum_sems.at[0])
    wait_for(r.decays.at[0, pl.ds(0, NZ - 1)], r.decay_sent)
    wait_for(r.decays.at[pl.ds(0, NX - 1)], r.decay_sent)
    for turn in range(2 * NX - 1):
        wait_for(r.w_all.at[turn % NX, :, 0], r.w_sent)
    wait_for(r.w_all.at[0, pl.ds(0, NZ - 1), 0], r.w_sent)


def leave_kernel(*refs):
    made, small, outs, gain, skip, sems = refs[:5], refs[5], refs[6:11], refs[11], refs[12], refs[13]
    for index in range(5):
        local(made[index], outs[index], sems.at[index]).start()
    pairs = skip.shape[0] // 2
    for pair in range(pairs):
        gain[pl.ds(pair * LANES, LANES)] = small[pair]
        line = small[pairs + pair : pairs + pair + 1]
        for side in (0, 1):
            skip[2 * pair + side] = jnp.sum(line[:, side * HDIM : (side + 1) * HDIM])
    for index in range(5):
        local(made[index], outs[index], sems.at[index]).wait()


def per_device(xin, zin, bmat, cmat, ldec, dskip, gain, w_out, dout):
    shape = jax.ShapeDtypeStruct
    dma = pltpu.SemaphoreType.DMA
    blocks, groups = lax.axis_size("ctx"), lax.axis_size("head")
    heads, tokens = ldec.shape
    inner, width = heads * HDIM, bmat.shape[1]
    rows, share = inner // blocks, tokens // groups
    piece = w_out.shape
    wide = pltpu.VMEM((tokens, inner), f32)
    wide_half = pltpu.VMEM((tokens, inner), bf16)
    narrow = pltpu.VMEM((tokens, LANES), f32)
    square = (heads, tokens, tokens)
    slices = pltpu.VMEM((blocks // NC, rows, width), f32)
    half_flat = pltpu.VMEM((inner // NC, width), f32)
    flat = pltpu.VMEM((inner, width), f32)
    operands = {
        "x": xin, "z": zin, "b": bmat, "c": cmat, "ldec": ldec,
        "dskip": dskip, "gain_in": gain, "w": w_out, "dout": dout,
    }
    outs = {
        "grad_x": shape((tokens, inner), bf16),
        "grad_z": shape((tokens, inner), bf16),
        "grad_b": shape((tokens, width), f32),
        "grad_c": shape((tokens, width), f32),
        "grad_w": shape(piece, f32),
        "small_total": shape((8, LANES), f32),
    }
    scratch = {
        "skip": pltpu.VMEM((1, inner), f32), "gain": pltpu.VMEM((1, inner), f32),
        "cum": pltpu.VMEM((heads, 1, tokens), f32), "col": pltpu.VMEM((heads, tokens, LANES), f32),
        "tail": wide, "inc": wide, "scores": pltpu.VMEM((tokens, tokens), f32),
        "decay": pltpu.VMEM(square, f32), "kern_high": pltpu.VMEM(square, bf16),
        "kern_low": pltpu.VMEM(square, bf16), "mixed": wide, "act": wide, "slope": wide, "gated": wide,
        "normed_grad": wide, "carried": wide, "grad": wide, "grad_inc": wide, "grad_values": wide,
        "normed_high": wide_half, "normed_low": wide_half, "square": narrow, "product": narrow,
        "inv": narrow, "pull": narrow, "products": pltpu.VMEM((tokens, tokens), f32),
        "part_b": narrow, "part_c": narrow,
        "pair_decays": pltpu.VMEM((NC, heads, 1, LANES), f32), "pair_sems": dma((2,)),
        "decays": pltpu.VMEM((NX, NZ, heads // NC, 1, LANES), f32), "decay_sent": dma(()),
        "decay_z": dma((NZ,)), "decay_x": dma((NX,)),
        "small": pltpu.VMEM((8, LANES), f32), "small_twin": pltpu.VMEM((8, LANES), f32),
        "small_z": pltpu.VMEM((NZ, 8, LANES), f32), "small_x": pltpu.VMEM((NX, 8, LANES), f32),
        "small_sems": dma((6,)),
        "w_all": pltpu.VMEM((NX, NZ, NC) + piece, bf16), "w_sent": dma(()), "w_z": dma((NZ,)),
        "w_x": dma((NX,)), "w_core": dma((NX,)), "w_own": dma(()),
        "dout_all": pltpu.VMEM((groups,) + dout.shape, bf16), "d_sent": dma(()),
        "d_came": dma((2, groups // 2 + 1)),
        "dout_turned": pltpu.VMEM((groups, dout.shape[1], tokens), bf16),
        "sums": pltpu.VMEM((8, tokens), f32), "sums_got": pltpu.VMEM((groups, 8, tokens), f32),
        "sum_sems": dma((2,)),
        "grads": pltpu.VMEM((NX, NZ, NC) + piece, f32), "twin_got": pltpu.VMEM((NX, NZ) + piece, f32),
        "mid": pltpu.VMEM((NX, NZ) + piece, f32), "x_got": pltpu.VMEM((NX - 1, NZ) + piece, f32),
        "low": pltpu.VMEM((NZ,) + piece, f32), "z_got": pltpu.VMEM((NZ,) + piece, f32),
        "twin_sems": dma((2, NX)), "x_sent": dma(()), "x_came": dma((PARTS, NX)), "z_sent": dma(()),
        "z_came": dma(()),
        "got_b": pltpu.VMEM((groups, share, width), f32), "sum_b": pltpu.VMEM((share, width), f32),
        "b_sems": dma((4,)),
        "got_c": pltpu.VMEM((groups, share, width), f32), "sum_c": pltpu.VMEM((share, width), f32),
        "c_sems": dma((4,)),
    }
    for name in ("fore", "back"):
        scratch |= {
            name + "_state": flat, name + "_came": flat, name + "_twin": half_flat, name + "_half": half_flat,
            name + "_got": slices, name + "_before": slices, name + "_entry": half_flat,
            name + "_give": half_flat, name + "_sems": dma((8,)),
        }
    names = tuple(operands) + tuple(outs) + tuple(scratch)
    vmem = pl.BlockSpec(memory_space=pltpu.VMEM)
    made = pl.pallas_call(
        lambda *refs: whole_kernel(names, *refs),
        out_shape=tuple(outs.values()),
        in_specs=[pl.BlockSpec(memory_space=pltpu.SMEM) if key == "dskip" else vmem for key in operands],
        out_specs=(vmem,) * len(outs),
        scratch_shapes=list(scratch.values()),
        name="whole",
        compiler_params=pltpu.CompilerParams(
            collective_id=0, has_side_effects=True, vmem_limit_bytes=VMEM_LIMIT
        ),
    )(*operands.values())
    anywhere = pl.BlockSpec(memory_space=pl.ANY)
    whole = tuple(outs.values())[:5]
    return pl.pallas_call(
        leave_kernel,
        out_shape=whole + (shape((inner,), f32), shape((heads,), f32)),
        in_specs=[vmem] * 6,
        out_specs=(anywhere,) * 5 + (vmem, pl.BlockSpec(memory_space=pltpu.SMEM)),
        scratch_shapes=[dma((5,))],
        name="leave",
    )(*made)


def solution(mesh):
    return jax.shard_map(
        per_device,
        mesh=mesh,
        in_specs=(
            P("ctx", "head"), P("ctx", "head"), P("ctx", None), P("ctx", None), P("head", "ctx"),
            P("head"), P("head"), P("ctx", "head"), P("ctx", "head"),
        ),
        out_specs=(
            P("ctx", "head"), P("ctx", "head"), P("ctx", None), P("ctx", None), P("ctx", "head"),
            P("head"), P("head"),
        ),
        check_vma=False,
    )
```

```python
import types
import jax
import jax.numpy as jnp
from jax import lax
from jax.experimental import pallas as pl
from jax.experimental.pallas import tpu as pltpu
from jax.sharding import PartitionSpec as P

HDIM = 64
HIGH = lax.Precision.HIGHEST
EPSILON = 1e-05
MESH = pl.DeviceIdType.MESH
NX, NZ, NC = 4, 8, 2
PARTS = 4
LANES = 128
CHUNK = 16
VMEM_LIMIT = 56 * 2**20
f32, bf16 = jnp.float32, jnp.bfloat16


def remote(src, dst, sent, came, **where):
    return pltpu.make_async_remote_copy(
        src_ref=src, dst_ref=dst, send_sem=sent, recv_sem=came, device_id=where, device_id_type=MESH
    )


def local(src, dst, sem):
    return pltpu.make_async_copy(src, dst, sem)


def wait_for(ref, sem):
    local(ref, ref, sem).wait()


def others(axis, act):
    count, mine = lax.axis_size(axis), lax.axis_index(axis)

    def turn(step, carry):
        act(lax.rem(mine + step, count))
        return carry

    lax.fori_loop(1, count, turn, 0)


def ctx_of(x, z, core):
    return (x * NZ + z) * NC + core


def split(value):
    high = value.astype(bf16)
    return high, (value - high.astype(f32)).astype(bf16)


def dot(a, b):
    return jnp.dot(a, b, preferred_element_type=f32)


def dot_nt(a, b, precision=None):
    return lax.dot_general(
        a, b, (((1,), (1,)), ((), ())), preferred_element_type=f32, precision=precision
    )


def rows_at(ref, index, rows):
    return ref.at[pl.ds(pl.multiple_of(index * rows, rows), rows)]


def loop(count, body):
    def turn(index, carry):
        body(index)
        return carry

    lax.fori_loop(0, count, turn, 0)


def chip_peers(act):
    mine = lax.axis_index("ctx")
    chips = NX * NZ

    def turn(step, carry):
        act(lax.rem(mine // NC + step, chips))
        return carry

    lax.fori_loop(1, chips, turn, 0)


def joined(own, other, is_first):
    return jnp.where(is_first, own, other), jnp.where(is_first, other, own)


class Scan:
    def __init__(self, r, name, backward):
        self.state, self.came = getattr(r, name + "_state"), getattr(r, name + "_came")
        self.twin, self.half = getattr(r, name + "_twin"), getattr(r, name + "_half")
        self.got, self.before = getattr(r, name + "_got"), getattr(r, name + "_before")
        self.entry, self.give = getattr(r, name + "_entry"), getattr(r, name + "_give")
        self.sems, self.r, self.backward = getattr(r, name + "_sems"), r, backward
        mine = lax.axis_index("ctx")
        self.core, self.chip = lax.rem(mine, NC), mine // NC
        self.first = NC - 1 if backward else 0
        self.is_first = self.core == self.first
        self.heads = self.half.shape[0] // HDIM

    def to_twin(self):
        rows = self.half.shape[0]
        remote(
            rows_at(self.state, 1 - self.core, rows), self.twin, self.sems.at[0], self.sems.at[1],
            ctx=self.chip * NC + 1 - self.core,
        ).start()

    def send(self):
        wait_for(self.twin, self.sems.at[1])
        for index in range(self.heads):
            at = pl.ds(index * HDIM, HDIM)
            from_state = pl.ds(pl.multiple_of(self.core * self.half.shape[0] + index * HDIM, HDIM), HDIM)
            first, second = joined(self.state[from_state], self.twin[at], self.is_first)
            factor = self.r.pair_decays[1 - self.first, self.core * self.heads + index]
            self.half[at] = factor * first + second
        rows = self.got.shape[1]
        chip_peers(
            lambda peer: remote(
                rows_at(self.half, peer, rows), self.got.at[self.chip], self.sems.at[2], self.sems.at[3],
                ctx=peer * NC + self.core,
            ).start()
        )
        local(rows_at(self.half, self.chip, rows), self.got.at[self.chip], self.sems.at[3]).start()

    def turn(self):
        chips, rows = self.got.shape[0], self.got.shape[1]
        head = self.chip // (HDIM // rows)
        wait_for(self.got, self.sems.at[3])

        def step(index, total):
            index = chips - 1 - index if self.backward else index
            self.before[index] = total
            return self.r.decays[index // NZ, lax.rem(index, NZ), head] * total + self.got[index]

        lax.fori_loop(0, chips, step, jnp.zeros(self.got.shape[1:], f32), unroll=4)
        home = rows_at(self.entry, self.chip, rows)
        chip_peers(
            lambda peer: remote(
                self.before.at[peer], home, self.sems.at[4], self.sems.at[5], ctx=peer * NC + self.core
            ).start()
        )
        local(self.before.at[self.chip], home, self.sems.at[5]).start()

    def share(self):
        wait_for(self.entry, self.sems.at[5])
        rows = self.half.shape[0]
        for index in range(self.heads):
            at = pl.ds(index * HDIM, HDIM)
            to = pl.ds(pl.multiple_of(self.core * rows + index * HDIM, HDIM), HDIM)
            entry = self.entry[at]
            first, _ = joined(self.state[to], self.twin[at], self.is_first)
            factor = self.r.pair_decays[self.first, self.core * self.heads + index]
            later = factor * entry + first
            self.came[to] = jnp.where(self.is_first, entry, later)
            self.give[at] = jnp.where(self.is_first, later, entry)
        remote(
            self.give, rows_at(self.came, self.core, rows), self.sems.at[6], self.sems.at[7],
            ctx=self.chip * NC + 1 - self.core,
        ).start()

    def finish(self):
        wait_for(self.give, self.sems.at[7])

    def drain(self):
        most = self.got.at[pl.ds(0, self.got.shape[0] - 1)]
        wait_for(self.twin, self.sems.at[0])
        wait_for(most, self.sems.at[2])
        wait_for(most, self.sems.at[4])
        wait_for(self.give, self.sems.at[6])


def shared_send(part, got, sems):
    mine, rows = lax.axis_index("head"), got.shape[1]
    others(
        "head",
        lambda peer: remote(rows_at(part, peer, rows), got.at[mine], sems.at[0], sems.at[1], head=peer).start(),
    )
    local(rows_at(part, mine, rows), got.at[mine], sems.at[1]).start()


def shared_turn(got, summed, total, sems):
    mine, rows = lax.axis_index("head"), got.shape[1]
    wait_for(got, sems.at[1])
    value = got[0]
    for index in range(1, got.shape[0]):
        value = value + got[index]
    summed[...] = value
    home = rows_at(total, mine, rows)
    others("head", lambda peer: remote(summed, home, sems.at[2], sems.at[3], head=peer).start())
    local(summed, home, sems.at[3]).start()


def shared_end(got, total, sems):
    peers = got.at[pl.ds(0, got.shape[0] - 1)]
    wait_for(total, sems.at[3])
    wait_for(peers, sems.at[0])
    wait_for(peers, sems.at[2])


def whole_kernel(names, *refs):
    r = types.SimpleNamespace(**dict(zip(names, refs)))
    mine, row = lax.axis_index("ctx"), lax.axis_index("head")
    groups = lax.axis_size("head")
    x, z, core = mine // (NZ * NC), lax.rem(mine // NC, NZ), lax.rem(mine, NC)
    twin = ctx_of(x, z, 1 - core)
    heads, tokens = r.ldec.shape
    pairs = heads // 2
    inner = heads * HDIM
    half = tokens // 2
    features = inner * groups
    chunks = tokens // CHUNK
    first_head = lax.broadcasted_iota(jnp.int32, (tokens, LANES), 1) < HDIM

    def pair_lanes(pair):
        return pl.ds(pl.multiple_of(pair * LANES, LANES), LANES)

    def chunk_rows(chunk):
        return pl.ds(pl.multiple_of(chunk * CHUNK, CHUNK), CHUNK)

    barrier = pltpu.get_barrier_semaphore()

    def greet(**where):
        pl.semaphore_signal(barrier, inc=1, device_id=where, device_id_type=MESH)

    greet(ctx=twin)
    chip_peers(lambda peer: greet(ctx=peer * NC + core))
    others("head", lambda peer: greet(head=peer))

    r.gain[...] = r.gain_in[...].reshape(1, inner)
    for pair in range(pairs):
        r.skip[:, pair * LANES : (pair + 1) * LANES] = jnp.where(
            first_head[:1], r.dskip[2 * pair], r.dskip[2 * pair + 1]
        )
    token_of = lax.broadcasted_iota(jnp.int32, (tokens, tokens), 0)
    other_of = lax.broadcasted_iota(jnp.int32, (tokens, tokens), 1)
    logs = dot_nt(r.ldec[...], (token_of >= other_of).astype(f32), HIGH)
    columns = jnp.transpose(logs)
    for head in range(heads):
        r.cum[head] = logs[head : head + 1]
        r.col[head] = jnp.broadcast_to(columns[:, head : head + 1], (tokens, LANES))
    for head in range(heads):
        r.pair_decays[core, head] = jnp.exp(r.col[head, tokens - 1 : tokens, :])

    def local_states(pair):
        lanes = pair_lanes(pair)
        log = jnp.where(first_head, r.col[2 * pair], r.col[2 * pair + 1])
        tail = jnp.exp(log[tokens - 1 :] - log)
        r.tail[:, lanes] = tail
        r.inc[:, lanes] = jnp.exp(log)
        high, low = split(jnp.transpose(r.x[:, lanes].astype(f32) * tail))
        r.fore_state[pl.ds(pl.multiple_of(pair * LANES, LANES), LANES)] = dot(high, r.b[...]) + dot(
            low, r.b[...]
        )

    loop(pairs, local_states)
    pl.semaphore_wait(barrier, NX * NZ + groups - 1)

    fore, back = Scan(r, "fore", False), Scan(r, "back", True)
    fore.to_twin()
    mine_decays = r.pair_decays.at[core]
    remote(mine_decays, mine_decays, r.pair_sems.at[0], r.pair_sems.at[1], ctx=twin).start()
    w_home = local(r.w, r.w_all.at[x, z, core], r.w_own)
    w_home.start()
    for step in range(1, NZ):
        peer = ctx_of(x, lax.rem(z + step, NZ), core)
        remote(r.w, r.w_all.at[x, z, core], r.w_sent, r.w_z.at[step], ctx=peer).start()
    for turn in range(NX - 1):
        peer = ctx_of(lax.rem(x + turn + 1, NX), z, core)
        remote(r.w, r.w_all.at[x, z, core], r.w_sent, r.w_x.at[turn], ctx=peer).start()
    right, left = lax.rem(row + 1, groups), lax.rem(row + groups - 1, groups)
    far, near = groups // 2, groups - 1 - groups // 2

    def ring(step):
        for side, most, target, back in ((0, far, right, -step), (1, near, left, step)):
            if step < most:
                piece = lax.rem(row + groups + back, groups)
                if step:
                    wait_for(r.dout_all.at[piece], r.d_came.at[side, step])
                source = r.dout_all.at[piece] if step else r.dout
                remote(
                    source, r.dout_all.at[piece], r.d_sent, r.d_came.at[side, step + 1], head=target
                ).start()

    ring(0)

    scores = dot_nt(r.c[...], r.b[...])
    r.scores[...] = scores
    causal = (
        lax.broadcasted_iota(jnp.int32, (half, half), 0)
        >= lax.broadcasted_iota(jnp.int32, (half, half), 1)
    )

    def inside(pair):
        lanes = pair_lanes(pair)
        parts = []
        for head in (2 * pair, 2 * pair + 1):
            outs = []
            for top in (0, 1):
                high, low = [], []
                at = pl.ds(top * half, half)
                for side in range(top + 1):
                    to = pl.ds(side * half, half)
                    gap = r.col[head, at, :] - r.cum[head, :, to]
                    if side == top:
                        decay = jnp.where(causal, jnp.exp(jnp.where(causal, gap, 0.0)), 0.0)
                    else:
                        decay = jnp.exp(gap)
                    r.decay[head, at, to] = decay
                    h, l = split(decay * r.scores[at, to])
                    r.kern_high[head, at, to] = h
                    r.kern_low[head, at, to] = l
                    high.append(h)
                    low.append(l)
                values = r.x[pl.ds(0, (top + 1) * half), lanes]
                outs.append(
                    dot(jnp.concatenate(high, axis=1), values) + dot(jnp.concatenate(low, axis=1), values)
                )
            parts.append(jnp.concatenate(outs, axis=0))
        r.mixed[:, lanes] = jnp.where(first_head, parts[0], parts[1]) + r.skip[:, lanes] * r.x[
            :, lanes
        ].astype(f32)

    def gate(chunk):
        at = chunk_rows(chunk)
        value = r.z[at, :].astype(f32)
        sigmoid = 1.0 / (1.0 + jnp.exp(-value))
        r.act[at, :] = value * sigmoid
        r.slope[at, :] = sigmoid * (1.0 + value * (1.0 - sigmoid))

    def relay(step):
        source = lax.rem(z + NZ - step, NZ)
        wait_for(r.w_all.at[x, source, core], r.w_z.at[step])
        for turn in range(NX - 1):
            peer = ctx_of(lax.rem(x + turn + 1, NX), z, core)
            piece = r.w_all.at[x, source, core]
            remote(piece, piece, r.w_sent, r.w_x.at[turn], ctx=peer).start()

    wait_for(r.pair_decays.at[1 - core], r.pair_sems.at[1])
    for index in range(heads // NC):
        head = core * (heads // NC) + index
        r.decays[x, z, index] = r.pair_decays[0, head] * r.pair_decays[1, head]
    for step in range(1, NZ):
        peer = ctx_of(x, lax.rem(z + step, NZ), core)
        remote(r.decays.at[x, z], r.decays.at[x, z], r.decay_sent, r.decay_z.at[step], ctx=peer).start()
    fore.send()
    loop(pairs // 2, inside)
    if far > 1:
        ring(1)
    for step in range(1, NZ):
        relay(step)
    if far > 2:
        ring(2)
    w_home.wait()
    mine_line = r.w_all.at[x, :, core]
    remote(mine_line, mine_line, r.w_sent, r.w_core.at[0], ctx=twin).start()
    for step in range(1, NZ):
        wait_for(r.decays.at[x, lax.rem(z + NZ - step, NZ)], r.decay_z.at[step])
    for step in range(1, NX):
        line = r.decays.at[x]
        remote(line, line, r.decay_sent, r.decay_x.at[step], ctx=ctx_of(lax.rem(x + step, NX), z, core)).start()
    for step in range(1, NX):
        wait_for(r.decays.at[lax.rem(x + NX - step, NX)], r.decay_x.at[step])
    fore.turn()
    lax.fori_loop(pairs // 2, pairs, lambda pair, carry: (inside(pair), carry)[1], 0)
    for step in range(3, far):
        ring(step)
    loop(chunks, gate)
    for turn in range(NX - 1):
        line = r.w_all.at[lax.rem(x + NX - turn - 1, NX), :, core]
        wait_for(line, r.w_x.at[turn])
        remote(line, line, r.w_sent, r.w_core.at[turn + 1], ctx=twin).start()
    r.dout_all[row] = r.dout[...]
    wait_for(r.dout_all.at[lax.rem(row + groups - far, groups)], r.d_came.at[0, far])
    if near:
        wait_for(r.dout_all.at[lax.rem(row + near, groups)], r.d_came.at[1, near])

    def turned(piece):
        r.dout_turned[piece] = jnp.transpose(r.dout_all[piece])

    loop(groups, turned)
    piece_rows, piece_width = r.w.shape[0], r.dout.shape[1]
    line_pieces = NZ * NC * piece_rows // piece_width

    for turn in range(NX):
        wait_for(r.w_all.at[lax.rem(x + NX - turn, NX), :, 1 - core], r.w_core.at[turn])
    r.normed_grad[...] = dot(
        jnp.concatenate([r.dout_all[piece] for piece in range(groups)], axis=1),
        r.w_all[...].reshape(groups * piece_width, inner),
    )

    fore.share()
    fore.finish()
    in_high, in_low = split(r.fore_came[...])
    r.carried[...] = dot_nt(r.c[...], in_high) + dot_nt(r.c[...], in_low)

    def gated_rows(chunk):
        at = chunk_rows(chunk)
        mixed = r.mixed[at, :] + r.carried[at, :] * r.inc[at, :]
        gated = mixed * r.act[at, :]
        r.mixed[at, :] = mixed
        r.gated[at, :] = gated
        r.square[at, :] = lane_fold(gated * gated)
        r.product[at, :] = lane_fold(r.gain[...] * r.normed_grad[at, :] * gated)

    def lane_fold(value):
        return sum(value[:, lane : lane + LANES] for lane in range(LANES, inner, LANES)) + value[:, :LANES]

    ones = jnp.ones((8, LANES), f32)

    def wide(value):
        return jnp.concatenate([value] * (inner // LANES), axis=1)

    loop(chunks, gated_rows)
    top_row = lax.broadcasted_iota(jnp.int32, (8, tokens), 0) == 0
    r.sums[...] = jnp.where(
        top_row, dot_nt(ones, r.square[...], HIGH), dot_nt(ones, r.product[...], HIGH)
    )
    others(
        "head",
        lambda peer: remote(r.sums, r.sums_got.at[row], r.sum_sems.at[0], r.sum_sems.at[1], head=peer).start(),
    )
    local(r.sums, r.sums_got.at[row], r.sum_sems.at[1]).start()
    wait_for(r.sums_got, r.sum_sems.at[1])
    total = r.sums_got[0]
    for index in range(1, groups):
        total = total + r.sums_got[index]
    total = total / features
    inv = lax.rsqrt(total[0:1] + EPSILON)
    pull = inv * inv * inv * total[1:2]
    both = jnp.transpose(jnp.where(top_row, inv, pull))
    r.inv[...] = jnp.broadcast_to(both[:, 0:1], (tokens, LANES))
    r.pull[...] = jnp.broadcast_to(both[:, 1:2], (tokens, LANES))

    def gradient_rows(chunk, sums):
        at = chunk_rows(chunk)
        inv, pull = wide(r.inv[at, :]), wide(r.pull[at, :])
        gated, normed_grad = r.gated[at, :], r.normed_grad[at, :]
        scaled = gated * inv
        r.normed_high[at, :], r.normed_low[at, :] = split(scaled * r.gain[...])
        gated_grad = inv * (r.gain[...] * normed_grad) - gated * pull
        grad = gated_grad * r.act[at, :]
        r.grad_z[at, :] = (gated_grad * r.mixed[at, :] * r.slope[at, :]).astype(bf16)
        r.grad[at, :] = grad
        r.grad_inc[at, :] = grad * r.inc[at, :]
        gain = normed_grad * scaled
        skip = grad * r.x[at, :].astype(f32)
        fold = lambda value: sum(value[at : at + 8] for at in range(8, CHUNK, 8)) + value[:8]
        return sums[0] + fold(gain), sums[1] + fold(skip)

    zero = jnp.zeros((8, inner), f32)
    gain_sum, skip_sum = lax.fori_loop(0, chunks, gradient_rows, (zero, zero))
    gain_sum = jnp.sum(gain_sum, axis=0, keepdims=True)
    skip_sum = jnp.sum(skip_sum, axis=0, keepdims=True)
    for index in range(pairs):
        lanes = slice(index * LANES, (index + 1) * LANES)
        r.small[index : index + 1, :] = gain_sum[:, lanes]
        r.small[pairs + index : pairs + index + 1, :] = skip_sum[:, lanes]

    def local_gradients(pair):
        lanes = pair_lanes(pair)
        high, low = split(jnp.transpose(r.grad_inc[:, lanes]))
        r.back_state[pl.ds(pl.multiple_of(pair * LANES, LANES), LANES)] = dot(high, r.c[...]) + dot(
            low, r.c[...]
        )

    loop(pairs, local_gradients)
    back.to_twin()

    ahead, across, behind = [lax.rem(x + step, NX) for step in range(1, NX)]
    order = [across, ahead, behind, x]
    depth = NZ // PARTS
    for step in range(NX):
        left_side = jnp.concatenate(
            [r.dout_turned[order[step] * line_pieces + index] for index in range(line_pieces)], axis=0
        )
        value = dot(left_side, r.normed_high[...]) + dot(left_side, r.normed_low[...])
        r.grads[order[step]] = value.reshape(NZ, NC, piece_rows, inner)
        remote(
            r.grads.at[order[step], :, 1 - core], r.twin_got.at[order[step]], r.twin_sems.at[0, step],
            r.twin_sems.at[1, step], ctx=twin,
        ).start()

    remote(r.small, r.small_twin, r.small_sems.at[0], r.small_sems.at[1], ctx=twin).start()
    back.send()
    wait_for(r.small_twin, r.small_sems.at[1])
    r.small_z[z] = r.small[...] + r.small_twin[...]
    for step in range(1, NZ):
        peer = ctx_of(x, lax.rem(z + step, NZ), core)
        remote(r.small_z.at[z], r.small_z.at[z], r.small_sems.at[2], r.small_sems.at[3], ctx=peer).start()
    def add_twin(step):
        wait_for(r.twin_got.at[order[step]], r.twin_sems.at[1, step])

        def add(index):
            r.mid[order[step], index] = (
                r.grads[order[step], index, core] + r.twin_got[order[step], index]
            )

        loop(NZ, add)

    add_twin(0)
    via = NZ // 2
    sides = ((0, ahead), (1, behind))
    for side, target in sides:
        remote(
            r.mid.at[across, pl.ds(side * via, via)], r.passing.at[side], r.pass_sems.at[0, side],
            r.pass_sems.at[1, side], ctx=ctx_of(target, z, core),
        ).start()

    def products(pair):
        lanes = pair_lanes(pair)
        grad = r.grad[:, lanes]
        high, low = split(grad)
        both = jnp.concatenate([high, low], axis=1)
        values = r.x[:, lanes].astype(f32)
        turned_high, turned_low = split(jnp.transpose(grad))
        outs = []
        for side in (0, 1):
            head = 2 * pair + side
            masked = jnp.where(first_head == (side == 0), values, 0.0).astype(bf16)
            masked = jnp.concatenate([masked, masked], axis=1)
            for top in (0, 1):
                at, to = pl.ds(top * half, half), pl.ds(0, (top + 1) * half)
                value = dot_nt(both[top * half : (top + 1) * half], masked[: (top + 1) * half])
                r.products[at, to] += value * r.decay[head, at, to]
            mine_high = turned_high[side * HDIM : (side + 1) * HDIM]
            mine_low = turned_low[side * HDIM : (side + 1) * HDIM]
            lines = []
            for to in (0, 1):
                at, lane = pl.ds(to * half, tokens - to * half), pl.ds(to * half, half)
                kern = r.kern_high[head, at, lane]
                lines.append(
                    dot(mine_high[:, to * half :], kern)
                    + dot(mine_low[:, to * half :], kern)
                    + dot(mine_high[:, to * half :], r.kern_low[head, at, lane])
                )
            outs.append(jnp.concatenate(lines, axis=1))
        r.grad_values[:, lanes] = jnp.transpose(jnp.concatenate(outs, axis=0)) + r.skip[:, lanes] * grad

    r.products[...] = jnp.zeros_like(r.products)
    loop(pairs, products)
    for step in range(1, NX):
        add_twin(step)

    def pass_on():
        for side, target in sides:
            wait_for(r.passing.at[side], r.pass_sems.at[1, side])

            def join(index):
                r.mid[target, side * via + index] += r.passing[side, index]

            loop(via, join)

    def along_x(part):
        block = pl.ds(part * depth, depth)
        for side, target in sides:
            remote(
                r.mid.at[target, block], r.x_got.at[side, block], r.x_sent, r.x_came.at[part, side],
                ctx=ctx_of(target, z, core),
            ).start()

    high, low = split(r.products[...])
    in_high, in_low = split(r.fore_came[...])
    out_high, out_low = split(r.grad_inc[...])
    r.part_c[...] = (
        dot(high, r.b[...]) + dot(low, r.b[...])
        + dot(out_high, in_high) + dot(out_low, in_high) + dot(out_high, in_low)
    )
    shared_send(r.part_c, r.got_c, r.c_sems)
    high, low = split(jnp.transpose(r.products[...]))
    r.part_b[...] = dot(high, r.c[...]) + dot(low, r.c[...])

    def fold_part(part):
        block = pl.ds(part * depth, depth)
        for side in (0, 1):
            wait_for(r.x_got.at[side, block], r.x_came.at[part, side])

        def fold(turn):
            index = lax.rem(z + turn + 1, NZ)

            @pl.when((index >= part * depth) & (index < (part + 1) * depth))
            def _():
                r.low[index] = r.mid[x, index] + r.x_got[0, index] + r.x_got[1, index]

                @pl.when(index != z)
                def _():
                    remote(
                        r.low.at[index], r.z_got.at[z], r.z_sent, r.z_came, ctx=ctx_of(x, index, core)
                    ).start()

        loop(NZ, fold)

    back.turn()
    pass_on()
    for part in range(PARTS):
        along_x(part)
    shared_turn(r.got_c, r.sum_c, r.grad_c, r.c_sems)

    fold_part(0)
    back.share()
    wait_for(r.small_z.at[pl.ds(0, NZ - 1)], r.small_sems.at[3])
    value = r.small_z[0]
    for index in range(1, NZ):
        value = value + r.small_z[index]
    r.small_x[x] = value
    for step in range(1, NX):
        peer = ctx_of(lax.rem(x + step, NX), z, core)
        remote(r.small_x.at[x], r.small_x.at[x], r.small_sems.at[4], r.small_sems.at[5], ctx=peer).start()
    back.finish()
    in_high, in_low = split(r.back_came[...])
    r.carried[...] = dot_nt(r.b[...], in_high) + dot_nt(r.b[...], in_low)

    def weigh(chunk):
        at = chunk_rows(chunk)
        tail = r.tail[at, :]
        r.grad_x[at, :] = (r.grad_values[at, :] + r.carried[at, :] * tail).astype(bf16)
        r.grad_inc[at, :] = r.x[at, :].astype(f32) * tail

    loop(chunks, weigh)
    out_high, out_low = split(r.grad_inc[...])
    r.part_b[...] += dot(out_high, in_high) + dot(out_low, in_high) + dot(out_high, in_low)
    shared_send(r.part_b, r.got_b, r.b_sems)
    for part in range(1, PARTS):
        fold_part(part)
        if part == PARTS - 1:
            shared_turn(r.got_b, r.sum_b, r.grad_b, r.b_sems)
    local(r.low.at[z], r.z_got.at[z], r.z_came).start()
    wait_for(r.small_x.at[pl.ds(0, NX - 1)], r.small_sems.at[5])
    value = r.small_x[0]
    for index in range(1, NX):
        value = value + r.small_x[index]
    r.small_total[...] = value
    wait_for(r.z_got, r.z_came)
    value = r.z_got[0]
    for index in range(1, NZ):
        value = value + r.z_got[index]
    r.grad_w[...] = value

    shared_end(r.got_c, r.grad_c, r.c_sems)
    shared_end(r.got_b, r.grad_b, r.b_sems)
    fore.drain()
    back.drain()
    wait_for(r.pair_decays.at[core], r.pair_sems.at[0])
    wait_for(r.small, r.small_sems.at[0])
    wait_for(r.small_z.at[pl.ds(0, NZ - 1)], r.small_sems.at[2])
    wait_for(r.small_x.at[pl.ds(0, NX - 1)], r.small_sems.at[4])
    for step in range(NX):
        wait_for(r.twin_got.at[step], r.twin_sems.at[0, step])
    for side in (0, 1):
        wait_for(r.x_got.at[side], r.x_sent)
        wait_for(r.passing.at[side], r.pass_sems.at[0, side])
    wait_for(r.z_got.at[pl.ds(0, NZ - 1)], r.z_sent)
    wait_for(r.dout_all.at[pl.ds(0, groups - 1)], r.d_sent)
    wait_for(r.sums_got.at[pl.ds(0, groups - 1)], r.sum_sems.at[0])
    wait_for(r.decays.at[0, pl.ds(0, NZ - 1)], r.decay_sent)
    wait_for(r.decays.at[pl.ds(0, NX - 1)], r.decay_sent)
    for turn in range(2 * NX - 1):
        wait_for(r.w_all.at[turn % NX, :, 0], r.w_sent)
    wait_for(r.w_all.at[0, pl.ds(0, NZ - 1), 0], r.w_sent)


def leave_kernel(*refs):
    made, small, outs, gain, skip, sems = refs[:5], refs[5], refs[6:11], refs[11], refs[12], refs[13]
    for index in range(5):
        local(made[index], outs[index], sems.at[index]).start()
    pairs = skip.shape[0] // 2
    for pair in range(pairs):
        gain[pl.ds(pair * LANES, LANES)] = small[pair]
        line = small[pairs + pair : pairs + pair + 1]
        for side in (0, 1):
            skip[2 * pair + side] = jnp.sum(line[:, side * HDIM : (side + 1) * HDIM])
    for index in range(5):
        local(made[index], outs[index], sems.at[index]).wait()


def per_device(xin, zin, bmat, cmat, ldec, dskip, gain, w_out, dout):
    shape = jax.ShapeDtypeStruct
    dma = pltpu.SemaphoreType.DMA
    blocks, groups = lax.axis_size("ctx"), lax.axis_size("head")
    heads, tokens = ldec.shape
    inner, width = heads * HDIM, bmat.shape[1]
    rows, share = inner // blocks, tokens // groups
    piece = w_out.shape
    wide = pltpu.VMEM((tokens, inner), f32)
    wide_half = pltpu.VMEM((tokens, inner), bf16)
    narrow = pltpu.VMEM((tokens, LANES), f32)
    square = (heads, tokens, tokens)
    slices = pltpu.VMEM((blocks // NC, rows, width), f32)
    half_flat = pltpu.VMEM((inner // NC, width), f32)
    flat = pltpu.VMEM((inner, width), f32)
    operands = {
        "x": xin, "z": zin, "b": bmat, "c": cmat, "ldec": ldec,
        "dskip": dskip, "gain_in": gain, "w": w_out, "dout": dout,
    }
    outs = {
        "grad_x": shape((tokens, inner), bf16),
        "grad_z": shape((tokens, inner), bf16),
        "grad_b": shape((tokens, width), f32),
        "grad_c": shape((tokens, width), f32),
        "grad_w": shape(piece, f32),
        "small_total": shape((8, LANES), f32),
    }
    scratch = {
        "skip": pltpu.VMEM((1, inner), f32), "gain": pltpu.VMEM((1, inner), f32),
        "cum": pltpu.VMEM((heads, 1, tokens), f32), "col": pltpu.VMEM((heads, tokens, LANES), f32),
        "tail": wide, "inc": wide, "scores": pltpu.VMEM((tokens, tokens), f32),
        "decay": pltpu.VMEM(square, f32), "kern_high": pltpu.VMEM(square, bf16),
        "kern_low": pltpu.VMEM(square, bf16), "mixed": wide, "act": wide, "slope": wide, "gated": wide,
        "normed_grad": wide, "carried": wide, "grad": wide, "grad_inc": wide, "grad_values": wide,
        "normed_high": wide_half, "normed_low": wide_half, "square": narrow, "product": narrow,
        "inv": narrow, "pull": narrow, "products": pltpu.VMEM((tokens, tokens), f32),
        "part_b": narrow, "part_c": narrow,
        "pair_decays": pltpu.VMEM((NC, heads, 1, LANES), f32), "pair_sems": dma((2,)),
        "decays": pltpu.VMEM((NX, NZ, heads // NC, 1, LANES), f32), "decay_sent": dma(()),
        "decay_z": dma((NZ,)), "decay_x": dma((NX,)),
        "small": pltpu.VMEM((8, LANES), f32), "small_twin": pltpu.VMEM((8, LANES), f32),
        "small_z": pltpu.VMEM((NZ, 8, LANES), f32), "small_x": pltpu.VMEM((NX, 8, LANES), f32),
        "small_sems": dma((6,)),
        "w_all": pltpu.VMEM((NX, NZ, NC) + piece, bf16), "w_sent": dma(()), "w_z": dma((NZ,)),
        "w_x": dma((NX,)), "w_core": dma((NX,)), "w_own": dma(()),
        "dout_all": pltpu.VMEM((groups,) + dout.shape, bf16), "d_sent": dma(()),
        "d_came": dma((2, groups // 2 + 1)),
        "dout_turned": pltpu.VMEM((groups, dout.shape[1], tokens), bf16),
        "sums": pltpu.VMEM((8, tokens), f32), "sums_got": pltpu.VMEM((groups, 8, tokens), f32),
        "sum_sems": dma((2,)),
        "grads": pltpu.VMEM((NX, NZ, NC) + piece, f32), "twin_got": pltpu.VMEM((NX, NZ) + piece, f32),
        "mid": pltpu.VMEM((NX, NZ) + piece, f32), "x_got": pltpu.VMEM((2, NZ) + piece, f32), "passing": pltpu.VMEM((2, NZ // 2) + piece, f32),
        "pass_sems": dma((2, 2)),
        "low": pltpu.VMEM((NZ,) + piece, f32), "z_got": pltpu.VMEM((NZ,) + piece, f32),
        "twin_sems": dma((2, NX)), "x_sent": dma(()), "x_came": dma((PARTS, NX)), "z_sent": dma(()),
        "z_came": dma(()),
        "got_b": pltpu.VMEM((groups, share, width), f32), "sum_b": pltpu.VMEM((share, width), f32),
        "b_sems": dma((4,)),
        "got_c": pltpu.VMEM((groups, share, width), f32), "sum_c": pltpu.VMEM((share, width), f32),
        "c_sems": dma((4,)),
    }
    for name in ("fore", "back"):
        scratch |= {
            name + "_state": flat, name + "_came": flat, name + "_twin": half_flat, name + "_half": half_flat,
            name + "_got": slices, name + "_before": slices, name + "_entry": half_flat,
            name + "_give": half_flat, name + "_sems": dma((8,)),
        }
    names = tuple(operands) + tuple(outs) + tuple(scratch)
    vmem = pl.BlockSpec(memory_space=pltpu.VMEM)
    made = pl.pallas_call(
        lambda *refs: whole_kernel(names, *refs),
        out_shape=tuple(outs.values()),
        in_specs=[pl.BlockSpec(memory_space=pltpu.SMEM) if key == "dskip" else vmem for key in operands],
        out_specs=(vmem,) * len(outs),
        scratch_shapes=list(scratch.values()),
        name="whole",
        compiler_params=pltpu.CompilerParams(
            collective_id=0, has_side_effects=True, vmem_limit_bytes=VMEM_LIMIT
        ),
    )(*operands.values())
    anywhere = pl.BlockSpec(memory_space=pl.ANY)
    whole = tuple(outs.values())[:5]
    return pl.pallas_call(
        leave_kernel,
        out_shape=whole + (shape((inner,), f32), shape((heads,), f32)),
        in_specs=[vmem] * 6,
        out_specs=(anywhere,) * 5 + (vmem, pl.BlockSpec(memory_space=pltpu.SMEM)),
        scratch_shapes=[dma((5,))],
        name="leave",
    )(*made)


def solution(mesh):
    return jax.shard_map(
        per_device,
        mesh=mesh,
        in_specs=(
            P("ctx", "head"), P("ctx", "head"), P("ctx", None), P("ctx", None), P("head", "ctx"),
            P("head"), P("head"), P("ctx", "head"), P("ctx", "head"),
        ),
        out_specs=(
            P("ctx", "head"), P("ctx", "head"), P("ctx", None), P("ctx", None), P("ctx", "head"),
            P("head"), P("head"),
        ),
        check_vma=False,
    )
```

```python
import types
import jax
import jax.numpy as jnp
from jax import lax
from jax.experimental import pallas as pl
from jax.experimental.pallas import tpu as pltpu
from jax.sharding import PartitionSpec as P

HDIM = 64
HIGH = lax.Precision.HIGHEST
EPSILON = 1e-05
MESH = pl.DeviceIdType.MESH
NX, NZ, NC = 4, 8, 2
PARTS = 4
LANES = 128
CHUNK = 16
VMEM_LIMIT = 56 * 2**20
f32, bf16 = jnp.float32, jnp.bfloat16


def remote(src, dst, sent, came, **where):
    return pltpu.make_async_remote_copy(
        src_ref=src, dst_ref=dst, send_sem=sent, recv_sem=came, device_id=where, device_id_type=MESH
    )


def local(src, dst, sem):
    return pltpu.make_async_copy(src, dst, sem)


def wait_for(ref, sem):
    local(ref, ref, sem).wait()


def others(axis, act):
    count, mine = lax.axis_size(axis), lax.axis_index(axis)

    def turn(step, carry):
        act(lax.rem(mine + step, count))
        return carry

    lax.fori_loop(1, count, turn, 0)


def ctx_of(x, z, core):
    return (x * NZ + z) * NC + core


def split(value):
    high = value.astype(bf16)
    return high, (value - high.astype(f32)).astype(bf16)


def dot(a, b):
    return jnp.dot(a, b, preferred_element_type=f32)


def dot_nt(a, b, precision=None):
    return lax.dot_general(
        a, b, (((1,), (1,)), ((), ())), preferred_element_type=f32, precision=precision
    )


def rows_at(ref, index, rows):
    return ref.at[pl.ds(pl.multiple_of(index * rows, rows), rows)]


def loop(count, body):
    def turn(index, carry):
        body(index)
        return carry

    lax.fori_loop(0, count, turn, 0)


def chip_peers(act):
    mine = lax.axis_index("ctx")
    chips = NX * NZ

    def turn(step, carry):
        act(lax.rem(mine // NC + step, chips))
        return carry

    lax.fori_loop(1, chips, turn, 0)


def joined(own, other, is_first):
    return jnp.where(is_first, own, other), jnp.where(is_first, other, own)


class Scan:
    def __init__(self, r, name, backward):
        self.state, self.came = getattr(r, name + "_state"), getattr(r, name + "_came")
        self.twin, self.half = getattr(r, name + "_twin"), getattr(r, name + "_half")
        self.got, self.before = getattr(r, name + "_got"), getattr(r, name + "_before")
        self.entry, self.give = getattr(r, name + "_entry"), getattr(r, name + "_give")
        self.sems, self.r, self.backward = getattr(r, name + "_sems"), r, backward
        mine = lax.axis_index("ctx")
        self.core, self.chip = lax.rem(mine, NC), mine // NC
        self.first = NC - 1 if backward else 0
        self.is_first = self.core == self.first
        self.heads = self.half.shape[0] // HDIM

    def to_twin(self):
        rows = self.half.shape[0]
        remote(
            rows_at(self.state, 1 - self.core, rows), self.twin, self.sems.at[0], self.sems.at[1],
            ctx=self.chip * NC + 1 - self.core,
        ).start()

    def send(self):
        wait_for(self.twin, self.sems.at[1])
        for index in range(self.heads):
            at = pl.ds(index * HDIM, HDIM)
            from_state = pl.ds(pl.multiple_of(self.core * self.half.shape[0] + index * HDIM, HDIM), HDIM)
            first, second = joined(self.state[from_state], self.twin[at], self.is_first)
            factor = self.r.pair_decays[1 - self.first, self.core * self.heads + index]
            self.half[at] = factor * first + second
        rows = self.got.shape[1]
        chip_peers(
            lambda peer: remote(
                rows_at(self.half, peer, rows), self.got.at[self.chip], self.sems.at[2], self.sems.at[3],
                ctx=peer * NC + self.core,
            ).start()
        )
        local(rows_at(self.half, self.chip, rows), self.got.at[self.chip], self.sems.at[3]).start()

    def turn(self):
        chips, rows = self.got.shape[0], self.got.shape[1]
        head = self.chip // (HDIM // rows)
        wait_for(self.got, self.sems.at[3])

        def step(index, total):
            index = chips - 1 - index if self.backward else index
            self.before[index] = total
            return self.r.decays[index // NZ, lax.rem(index, NZ), head] * total + self.got[index]

        lax.fori_loop(0, chips, step, jnp.zeros(self.got.shape[1:], f32), unroll=4)
        home = rows_at(self.entry, self.chip, rows)
        chip_peers(
            lambda peer: remote(
                self.before.at[peer], home, self.sems.at[4], self.sems.at[5], ctx=peer * NC + self.core
            ).start()
        )
        local(self.before.at[self.chip], home, self.sems.at[5]).start()

    def share(self):
        wait_for(self.entry, self.sems.at[5])
        rows = self.half.shape[0]
        for index in range(self.heads):
            at = pl.ds(index * HDIM, HDIM)
            to = pl.ds(pl.multiple_of(self.core * rows + index * HDIM, HDIM), HDIM)
            entry = self.entry[at]
            first, _ = joined(self.state[to], self.twin[at], self.is_first)
            factor = self.r.pair_decays[self.first, self.core * self.heads + index]
            later = factor * entry + first
            self.came[to] = jnp.where(self.is_first, entry, later)
            self.give[at] = jnp.where(self.is_first, later, entry)
        remote(
            self.give, rows_at(self.came, self.core, rows), self.sems.at[6], self.sems.at[7],
            ctx=self.chip * NC + 1 - self.core,
        ).start()

    def finish(self):
        wait_for(self.give, self.sems.at[7])

    def drain(self):
        most = self.got.at[pl.ds(0, self.got.shape[0] - 1)]
        wait_for(self.twin, self.sems.at[0])
        wait_for(most, self.sems.at[2])
        wait_for(most, self.sems.at[4])
        wait_for(self.give, self.sems.at[6])


def shared_send(part, got, sems):
    mine, rows = lax.axis_index("head"), got.shape[1]
    others(
        "head",
        lambda peer: remote(rows_at(part, peer, rows), got.at[mine], sems.at[0], sems.at[1], head=peer).start(),
    )
    local(rows_at(part, mine, rows), got.at[mine], sems.at[1]).start()


def shared_turn(got, summed, total, sems):
    mine, rows = lax.axis_index("head"), got.shape[1]
    wait_for(got, sems.at[1])
    value = got[0]
    for index in range(1, got.shape[0]):
        value = value + got[index]
    summed[...] = value
    home = rows_at(total, mine, rows)
    others("head", lambda peer: remote(summed, home, sems.at[2], sems.at[3], head=peer).start())
    local(summed, home, sems.at[3]).start()


def shared_end(got, total, sems):
    peers = got.at[pl.ds(0, got.shape[0] - 1)]
    wait_for(total, sems.at[3])
    wait_for(peers, sems.at[0])
    wait_for(peers, sems.at[2])


def whole_kernel(names, *refs):
    r = types.SimpleNamespace(**dict(zip(names, refs)))
    mine, row = lax.axis_index("ctx"), lax.axis_index("head")
    groups = lax.axis_size("head")
    x, z, core = mine // (NZ * NC), lax.rem(mine // NC, NZ), lax.rem(mine, NC)
    twin = ctx_of(x, z, 1 - core)
    heads, tokens = r.ldec.shape
    pairs = heads // 2
    inner = heads * HDIM
    half = tokens // 2
    features = inner * groups
    chunks = tokens // CHUNK
    first_head = lax.broadcasted_iota(jnp.int32, (tokens, LANES), 1) < HDIM

    def pair_lanes(pair):
        return pl.ds(pl.multiple_of(pair * LANES, LANES), LANES)

    def chunk_rows(chunk):
        return pl.ds(pl.multiple_of(chunk * CHUNK, CHUNK), CHUNK)

    barrier = pltpu.get_barrier_semaphore()

    def greet(**where):
        pl.semaphore_signal(barrier, inc=1, device_id=where, device_id_type=MESH)

    greet(ctx=twin)
    chip_peers(lambda peer: greet(ctx=peer * NC + core))
    others("head", lambda peer: greet(head=peer))

    r.gain[...] = r.gain_in[...].reshape(1, inner)
    for pair in range(pairs):
        r.skip[:, pair * LANES : (pair + 1) * LANES] = jnp.where(
            first_head[:1], r.dskip[2 * pair], r.dskip[2 * pair + 1]
        )
    token_of = lax.broadcasted_iota(jnp.int32, (tokens, tokens), 0)
    other_of = lax.broadcasted_iota(jnp.int32, (tokens, tokens), 1)
    logs = dot_nt(r.ldec[...], (token_of >= other_of).astype(f32), HIGH)
    columns = jnp.transpose(logs)
    for head in range(heads):
        r.cum[head] = logs[head : head + 1]
        r.col[head] = jnp.broadcast_to(columns[:, head : head + 1], (tokens, LANES))
    for head in range(heads):
        r.pair_decays[core, head] = jnp.exp(r.col[head, tokens - 1 : tokens, :])

    def local_states(pair):
        lanes = pair_lanes(pair)
        log = jnp.where(first_head, r.col[2 * pair], r.col[2 * pair + 1])
        tail = jnp.exp(log[tokens - 1 :] - log)
        r.tail[:, lanes] = tail
        r.inc[:, lanes] = jnp.exp(log)
        high, low = split(jnp.transpose(r.x[:, lanes].astype(f32) * tail))
        r.fore_state[pl.ds(pl.multiple_of(pair * LANES, LANES), LANES)] = dot(high, r.b[...]) + dot(
            low, r.b[...]
        )

    loop(pairs, local_states)
    pl.semaphore_wait(barrier, NX * NZ + groups - 1)

    fore, back = Scan(r, "fore", False), Scan(r, "back", True)
    fore.to_twin()
    mine_decays = r.pair_decays.at[core]
    remote(mine_decays, mine_decays, r.pair_sems.at[0], r.pair_sems.at[1], ctx=twin).start()
    w_home = local(r.w, r.w_all.at[x, z, core], r.w_own)
    w_home.start()
    for step in range(1, NZ):
        peer = ctx_of(x, lax.rem(z + step, NZ), core)
        remote(r.w, r.w_all.at[x, z, core], r.w_sent, r.w_z.at[step], ctx=peer).start()
    for turn in range(NX - 1):
        peer = ctx_of(lax.rem(x + turn + 1, NX), z, core)
        remote(r.w, r.w_all.at[x, z, core], r.w_sent, r.w_x.at[turn], ctx=peer).start()
    right, left = lax.rem(row + 1, groups), lax.rem(row + groups - 1, groups)
    far, near = groups // 2, groups - 1 - groups // 2

    def ring(step):
        for side, most, target, back in ((0, far, right, -step), (1, near, left, step)):
            if step < most:
                piece = lax.rem(row + groups + back, groups)
                if step:
                    wait_for(r.dout_all.at[piece], r.d_came.at[side, step])
                source = r.dout_all.at[piece] if step else r.dout
                remote(
                    source, r.dout_all.at[piece], r.d_sent, r.d_came.at[side, step + 1], head=target
                ).start()

    ring(0)

    scores = dot_nt(r.c[...], r.b[...])
    r.scores[...] = scores
    causal = (
        lax.broadcasted_iota(jnp.int32, (half, half), 0)
        >= lax.broadcasted_iota(jnp.int32, (half, half), 1)
    )

    def inside(pair):
        lanes = pair_lanes(pair)
        parts = []
        for head in (2 * pair, 2 * pair + 1):
            outs = []
            for top in (0, 1):
                high, low = [], []
                at = pl.ds(top * half, half)
                for side in range(top + 1):
                    to = pl.ds(side * half, half)
                    gap = r.col[head, at, :] - r.cum[head, :, to]
                    if side == top:
                        decay = jnp.where(causal, jnp.exp(jnp.where(causal, gap, 0.0)), 0.0)
                    else:
                        decay = jnp.exp(gap)
                    r.decay[head, at, to] = decay
                    h, l = split(decay * r.scores[at, to])
                    r.kern_high[head, at, to] = h
                    r.kern_low[head, at, to] = l
                    high.append(h)
                    low.append(l)
                values = r.x[pl.ds(0, (top + 1) * half), lanes]
                outs.append(
                    dot(jnp.concatenate(high, axis=1), values) + dot(jnp.concatenate(low, axis=1), values)
                )
            parts.append(jnp.concatenate(outs, axis=0))
        r.mixed[:, lanes] = jnp.where(first_head, parts[0], parts[1]) + r.skip[:, lanes] * r.x[
            :, lanes
        ].astype(f32)

    def gate(chunk):
        at = chunk_rows(chunk)
        value = r.z[at, :].astype(f32)
        sigmoid = 1.0 / (1.0 + jnp.exp(-value))
        r.act[at, :] = value * sigmoid
        r.slope[at, :] = sigmoid * (1.0 + value * (1.0 - sigmoid))

    def relay(step):
        source = lax.rem(z + NZ - step, NZ)
        wait_for(r.w_all.at[x, source, core], r.w_z.at[step])
        for turn in range(NX - 1):
            peer = ctx_of(lax.rem(x + turn + 1, NX), z, core)
            piece = r.w_all.at[x, source, core]
            remote(piece, piece, r.w_sent, r.w_x.at[turn], ctx=peer).start()

    wait_for(r.pair_decays.at[1 - core], r.pair_sems.at[1])
    for index in range(heads // NC):
        head = core * (heads // NC) + index
        r.decays[x, z, index] = r.pair_decays[0, head] * r.pair_decays[1, head]
    for step in range(1, NZ):
        peer = ctx_of(x, lax.rem(z + step, NZ), core)
        remote(r.decays.at[x, z], r.decays.at[x, z], r.decay_sent, r.decay_z.at[step], ctx=peer).start()
    fore.send()
    loop(pairs // 2, inside)
    if far > 1:
        ring(1)
    for step in range(1, NZ):
        relay(step)
    if far > 2:
        ring(2)
    w_home.wait()
    mine_line = r.w_all.at[x, :, core]
    remote(mine_line, mine_line, r.w_sent, r.w_core.at[0], ctx=twin).start()
    for step in range(1, NZ):
        wait_for(r.decays.at[x, lax.rem(z + NZ - step, NZ)], r.decay_z.at[step])
    for step in range(1, NX):
        line = r.decays.at[x]
        remote(line, line, r.decay_sent, r.decay_x.at[step], ctx=ctx_of(lax.rem(x + step, NX), z, core)).start()
    for step in range(1, NX):
        wait_for(r.decays.at[lax.rem(x + NX - step, NX)], r.decay_x.at[step])
    fore.turn()
    lax.fori_loop(pairs // 2, pairs, lambda pair, carry: (inside(pair), carry)[1], 0)
    for step in range(3, far):
        ring(step)
    loop(chunks, gate)
    for turn in range(NX - 1):
        line = r.w_all.at[lax.rem(x + NX - turn - 1, NX), :, core]
        wait_for(line, r.w_x.at[turn])
        remote(line, line, r.w_sent, r.w_core.at[turn + 1], ctx=twin).start()
    r.dout_all[row] = r.dout[...]
    wait_for(r.dout_all.at[lax.rem(row + groups - far, groups)], r.d_came.at[0, far])
    if near:
        wait_for(r.dout_all.at[lax.rem(row + near, groups)], r.d_came.at[1, near])

    def turned(piece):
        r.dout_turned[piece] = jnp.transpose(r.dout_all[piece])

    loop(groups, turned)
    piece_rows, piece_width = r.w.shape[0], r.dout.shape[1]
    line_pieces = NZ * NC * piece_rows // piece_width

    for turn in range(NX):
        wait_for(r.w_all.at[lax.rem(x + NX - turn, NX), :, 1 - core], r.w_core.at[turn])
    r.normed_grad[...] = dot(
        jnp.concatenate([r.dout_all[piece] for piece in range(groups)], axis=1),
        r.w_all[...].reshape(groups * piece_width, inner),
    )

    fore.share()
    fore.finish()
    in_high, in_low = split(r.fore_came[...])
    r.carried[...] = dot_nt(r.c[...], in_high) + dot_nt(r.c[...], in_low)

    def gated_rows(chunk):
        at = chunk_rows(chunk)
        mixed = r.mixed[at, :] + r.carried[at, :] * r.inc[at, :]
        gated = mixed * r.act[at, :]
        r.mixed[at, :] = mixed
        r.gated[at, :] = gated
        r.square[at, :] = lane_fold(gated * gated)
        r.product[at, :] = lane_fold(r.gain[...] * r.normed_grad[at, :] * gated)

    def lane_fold(value):
        return sum(value[:, lane : lane + LANES] for lane in range(LANES, inner, LANES)) + value[:, :LANES]

    ones = jnp.ones((8, LANES), f32)

    def wide(value):
        return jnp.concatenate([value] * (inner // LANES), axis=1)

    loop(chunks, gated_rows)
    top_row = lax.broadcasted_iota(jnp.int32, (8, tokens), 0) == 0
    r.sums[...] = jnp.where(
        top_row, dot_nt(ones, r.square[...], HIGH), dot_nt(ones, r.product[...], HIGH)
    )
    others(
        "head",
        lambda peer: remote(r.sums, r.sums_got.at[row], r.sum_sems.at[0], r.sum_sems.at[1], head=peer).start(),
    )
    local(r.sums, r.sums_got.at[row], r.sum_sems.at[1]).start()
    wait_for(r.sums_got, r.sum_sems.at[1])
    total = r.sums_got[0]
    for index in range(1, groups):
        total = total + r.sums_got[index]
    total = total / features
    inv = lax.rsqrt(total[0:1] + EPSILON)
    pull = inv * inv * inv * total[1:2]
    both = jnp.transpose(jnp.where(top_row, inv, pull))
    r.inv[...] = jnp.broadcast_to(both[:, 0:1], (tokens, LANES))
    r.pull[...] = jnp.broadcast_to(both[:, 1:2], (tokens, LANES))

    def gradient_rows(chunk, sums):
        at = chunk_rows(chunk)
        inv, pull = wide(r.inv[at, :]), wide(r.pull[at, :])
        gated, normed_grad = r.gated[at, :], r.normed_grad[at, :]
        scaled = gated * inv
        r.normed_high[at, :], r.normed_low[at, :] = split(scaled * r.gain[...])
        gated_grad = inv * (r.gain[...] * normed_grad) - gated * pull
        grad = gated_grad * r.act[at, :]
        r.grad_z[at, :] = (gated_grad * r.mixed[at, :] * r.slope[at, :]).astype(bf16)
        r.grad[at, :] = grad
        r.grad_inc[at, :] = grad * r.inc[at, :]
        gain = normed_grad * scaled
        skip = grad * r.x[at, :].astype(f32)
        fold = lambda value: sum(value[at : at + 8] for at in range(8, CHUNK, 8)) + value[:8]
        return sums[0] + fold(gain), sums[1] + fold(skip)

    zero = jnp.zeros((8, inner), f32)
    gain_sum, skip_sum = lax.fori_loop(0, chunks, gradient_rows, (zero, zero))
    gain_sum = jnp.sum(gain_sum, axis=0, keepdims=True)
    skip_sum = jnp.sum(skip_sum, axis=0, keepdims=True)
    for index in range(pairs):
        lanes = slice(index * LANES, (index + 1) * LANES)
        r.small[index : index + 1, :] = gain_sum[:, lanes]
        r.small[pairs + index : pairs + index + 1, :] = skip_sum[:, lanes]

    def local_gradients(pair):
        lanes = pair_lanes(pair)
        high, low = split(jnp.transpose(r.grad_inc[:, lanes]))
        r.back_state[pl.ds(pl.multiple_of(pair * LANES, LANES), LANES)] = dot(high, r.c[...]) + dot(
            low, r.c[...]
        )

    loop(pairs, local_gradients)
    back.to_twin()

    ahead, across, behind = [lax.rem(x + step, NX) for step in range(1, NX)]
    order = [across, ahead, behind, x]
    depth = NZ // PARTS
    for step in range(NX):
        left_side = jnp.concatenate(
            [r.dout_turned[order[step] * line_pieces + index] for index in range(line_pieces)], axis=0
        )
        value = dot(left_side, r.normed_high[...]) + dot(left_side, r.normed_low[...])
        r.grads[order[step]] = value.reshape(NZ, NC, piece_rows, inner)
        remote(
            r.grads.at[order[step], :, 1 - core], r.twin_got.at[order[step]], r.twin_sems.at[0, step],
            r.twin_sems.at[1, step], ctx=twin,
        ).start()

    remote(r.small, r.small_twin, r.small_sems.at[0], r.small_sems.at[1], ctx=twin).start()
    back.send()
    wait_for(r.small_twin, r.small_sems.at[1])
    r.small_z[z] = r.small[...] + r.small_twin[...]
    for step in range(1, NZ):
        peer = ctx_of(x, lax.rem(z + step, NZ), core)
        remote(r.small_z.at[z], r.small_z.at[z], r.small_sems.at[2], r.small_sems.at[3], ctx=peer).start()
    def add_twin(step):
        wait_for(r.twin_got.at[order[step]], r.twin_sems.at[1, step])

        def add(index):
            r.mid[order[step], index] = (
                r.grads[order[step], index, core] + r.twin_got[order[step], index]
            )

        loop(NZ, add)

    add_twin(0)
    via = NZ // 2
    sides = ((0, ahead), (1, behind))
    for side, target in sides:
        remote(
            r.mid.at[across, pl.ds(side * via, via)], r.passing.at[side], r.pass_sems.at[0, side],
            r.pass_sems.at[1, side], ctx=ctx_of(target, z, core),
        ).start()

    def products(pair):
        lanes = pair_lanes(pair)
        grad = r.grad[:, lanes]
        high, low = split(grad)
        both = jnp.concatenate([high, low], axis=1)
        values = r.x[:, lanes].astype(f32)
        turned_high, turned_low = split(jnp.transpose(grad))
        outs = []
        for side in (0, 1):
            head = 2 * pair + side
            masked = jnp.where(first_head == (side == 0), values, 0.0).astype(bf16)
            masked = jnp.concatenate([masked, masked], axis=1)
            for top in (0, 1):
                at, to = pl.ds(top * half, half), pl.ds(0, (top + 1) * half)
                value = dot_nt(both[top * half : (top + 1) * half], masked[: (top + 1) * half])
                r.products[at, to] += value * r.decay[head, at, to]
            mine_high = turned_high[side * HDIM : (side + 1) * HDIM]
            mine_low = turned_low[side * HDIM : (side + 1) * HDIM]
            lines = []
            for to in (0, 1):
                at, lane = pl.ds(to * half, tokens - to * half), pl.ds(to * half, half)
                kern = r.kern_high[head, at, lane]
                lines.append(
                    dot(mine_high[:, to * half :], kern)
                    + dot(mine_low[:, to * half :], kern)
                    + dot(mine_high[:, to * half :], r.kern_low[head, at, lane])
                )
            outs.append(jnp.concatenate(lines, axis=1))
        r.grad_values[:, lanes] = jnp.transpose(jnp.concatenate(outs, axis=0)) + r.skip[:, lanes] * grad

    r.products[...] = jnp.zeros_like(r.products)
    loop(pairs, products)
    for step in range(1, NX):
        add_twin(step)

    def pass_on():
        for side, target in sides:
            wait_for(r.passing.at[side], r.pass_sems.at[1, side])

            def join(index):
                r.mid[target, side * via + index] += r.passing[side, index]

            loop(via, join)

    def along_x(part):
        block = pl.ds(part * depth, depth)
        for side, target in sides:
            remote(
                r.mid.at[target, block], r.x_got.at[side, block], r.x_sent, r.x_came.at[part, side],
                ctx=ctx_of(target, z, core),
            ).start()

    high, low = split(r.products[...])
    in_high, in_low = split(r.fore_came[...])
    out_high, out_low = split(r.grad_inc[...])
    r.part_c[...] = (
        dot(high, r.b[...]) + dot(low, r.b[...])
        + dot(out_high, in_high) + dot(out_low, in_high) + dot(out_high, in_low)
    )
    shared_send(r.part_c, r.got_c, r.c_sems)
    high, low = split(jnp.transpose(r.products[...]))
    r.part_b[...] = dot(high, r.c[...]) + dot(low, r.c[...])

    def fold_part(part):
        block = pl.ds(part * depth, depth)
        for side in (0, 1):
            wait_for(r.x_got.at[side, block], r.x_came.at[part, side])

        def fold(turn):
            index = lax.rem(z + turn + 1, NZ)

            @pl.when((index >= part * depth) & (index < (part + 1) * depth))
            def _():
                r.low[index] = r.mid[x, index] + r.x_got[0, index] + r.x_got[1, index]

                @pl.when(index != z)
                def _():
                    remote(
                        r.low.at[index], r.z_got.at[z], r.z_sent, r.z_came, ctx=ctx_of(x, index, core)
                    ).start()

        loop(NZ, fold)

    back.turn()
    pass_on()
    for part in range(PARTS):
        along_x(part)
    shared_turn(r.got_c, r.sum_c, r.grad_c, r.c_sems)

    back.share()
    wait_for(r.small_z.at[pl.ds(0, NZ - 1)], r.small_sems.at[3])
    value = r.small_z[0]
    for index in range(1, NZ):
        value = value + r.small_z[index]
    r.small_x[x] = value
    for step in range(1, NX):
        peer = ctx_of(lax.rem(x + step, NX), z, core)
        remote(r.small_x.at[x], r.small_x.at[x], r.small_sems.at[4], r.small_sems.at[5], ctx=peer).start()
    fold_part(0)
    back.finish()
    in_high, in_low = split(r.back_came[...])
    r.carried[...] = dot_nt(r.b[...], in_high) + dot_nt(r.b[...], in_low)

    def weigh(chunk):
        at = chunk_rows(chunk)
        tail = r.tail[at, :]
        r.grad_x[at, :] = (r.grad_values[at, :] + r.carried[at, :] * tail).astype(bf16)
        r.grad_inc[at, :] = r.x[at, :].astype(f32) * tail

    loop(chunks, weigh)
    out_high, out_low = split(r.grad_inc[...])
    r.part_b[...] += dot(out_high, in_high) + dot(out_low, in_high) + dot(out_high, in_low)
    shared_send(r.part_b, r.got_b, r.b_sems)
    for part in range(1, PARTS):
        fold_part(part)
    shared_turn(r.got_b, r.sum_b, r.grad_b, r.b_sems)
    local(r.low.at[z], r.z_got.at[z], r.z_came).start()
    wait_for(r.small_x.at[pl.ds(0, NX - 1)], r.small_sems.at[5])
    value = r.small_x[0]
    for index in range(1, NX):
        value = value + r.small_x[index]
    r.small_total[...] = value
    wait_for(r.z_got, r.z_came)
    value = r.z_got[0]
    for index in range(1, NZ):
        value = value + r.z_got[index]
    r.grad_w[...] = value

    shared_end(r.got_c, r.grad_c, r.c_sems)
    shared_end(r.got_b, r.grad_b, r.b_sems)
    fore.drain()
    back.drain()
    wait_for(r.pair_decays.at[core], r.pair_sems.at[0])
    wait_for(r.small, r.small_sems.at[0])
    wait_for(r.small_z.at[pl.ds(0, NZ - 1)], r.small_sems.at[2])
    wait_for(r.small_x.at[pl.ds(0, NX - 1)], r.small_sems.at[4])
    for step in range(NX):
        wait_for(r.twin_got.at[step], r.twin_sems.at[0, step])
    for side in (0, 1):
        wait_for(r.x_got.at[side], r.x_sent)
        wait_for(r.passing.at[side], r.pass_sems.at[0, side])
    wait_for(r.z_got.at[pl.ds(0, NZ - 1)], r.z_sent)
    wait_for(r.dout_all.at[pl.ds(0, groups - 1)], r.d_sent)
    wait_for(r.sums_got.at[pl.ds(0, groups - 1)], r.sum_sems.at[0])
    wait_for(r.decays.at[0, pl.ds(0, NZ - 1)], r.decay_sent)
    wait_for(r.decays.at[pl.ds(0, NX - 1)], r.decay_sent)
    for turn in range(2 * NX - 1):
        wait_for(r.w_all.at[turn % NX, :, 0], r.w_sent)
    wait_for(r.w_all.at[0, pl.ds(0, NZ - 1), 0], r.w_sent)


def leave_kernel(*refs):
    made, small, outs, gain, skip, sems = refs[:5], refs[5], refs[6:11], refs[11], refs[12], refs[13]
    for index in range(5):
        local(made[index], outs[index], sems.at[index]).start()
    pairs = skip.shape[0] // 2
    for pair in range(pairs):
        gain[pl.ds(pair * LANES, LANES)] = small[pair]
        line = small[pairs + pair : pairs + pair + 1]
        for side in (0, 1):
            skip[2 * pair + side] = jnp.sum(line[:, side * HDIM : (side + 1) * HDIM])
    for index in range(5):
        local(made[index], outs[index], sems.at[index]).wait()


def per_device(xin, zin, bmat, cmat, ldec, dskip, gain, w_out, dout):
    shape = jax.ShapeDtypeStruct
    dma = pltpu.SemaphoreType.DMA
    blocks, groups = lax.axis_size("ctx"), lax.axis_size("head")
    heads, tokens = ldec.shape
    inner, width = heads * HDIM, bmat.shape[1]
    rows, share = inner // blocks, tokens // groups
    piece = w_out.shape
    wide = pltpu.VMEM((tokens, inner), f32)
    wide_half = pltpu.VMEM((tokens, inner), bf16)
    narrow = pltpu.VMEM((tokens, LANES), f32)
    square = (heads, tokens, tokens)
    slices = pltpu.VMEM((blocks // NC, rows, width), f32)
    half_flat = pltpu.VMEM((inner // NC, width), f32)
    flat = pltpu.VMEM((inner, width), f32)
    operands = {
        "x": xin, "z": zin, "b": bmat, "c": cmat, "ldec": ldec,
        "dskip": dskip, "gain_in": gain, "w": w_out, "dout": dout,
    }
    outs = {
        "grad_x": shape((tokens, inner), bf16),
        "grad_z": shape((tokens, inner), bf16),
        "grad_b": shape((tokens, width), f32),
        "grad_c": shape((tokens, width), f32),
        "grad_w": shape(piece, f32),
        "small_total": shape((8, LANES), f32),
    }
    scratch = {
        "skip": pltpu.VMEM((1, inner), f32), "gain": pltpu.VMEM((1, inner), f32),
        "cum": pltpu.VMEM((heads, 1, tokens), f32), "col": pltpu.VMEM((heads, tokens, LANES), f32),
        "tail": wide, "inc": wide, "scores": pltpu.VMEM((tokens, tokens), f32),
        "decay": pltpu.VMEM(square, f32), "kern_high": pltpu.VMEM(square, bf16),
        "kern_low": pltpu.VMEM(square, bf16), "mixed": wide, "act": wide, "slope": wide, "gated": wide,
        "normed_grad": wide, "carried": wide, "grad": wide, "grad_inc": wide, "grad_values": wide,
        "normed_high": wide_half, "normed_low": wide_half, "square": narrow, "product": narrow,
        "inv": narrow, "pull": narrow, "products": pltpu.VMEM((tokens, tokens), f32),
        "part_b": narrow, "part_c": narrow,
        "pair_decays": pltpu.VMEM((NC, heads, 1, LANES), f32), "pair_sems": dma((2,)),
        "decays": pltpu.VMEM((NX, NZ, heads // NC, 1, LANES), f32), "decay_sent": dma(()),
        "decay_z": dma((NZ,)), "decay_x": dma((NX,)),
        "small": pltpu.VMEM((8, LANES), f32), "small_twin": pltpu.VMEM((8, LANES), f32),
        "small_z": pltpu.VMEM((NZ, 8, LANES), f32), "small_x": pltpu.VMEM((NX, 8, LANES), f32),
        "small_sems": dma((6,)),
        "w_all": pltpu.VMEM((NX, NZ, NC) + piece, bf16), "w_sent": dma(()), "w_z": dma((NZ,)),
        "w_x": dma((NX,)), "w_core": dma((NX,)), "w_own": dma(()),
        "dout_all": pltpu.VMEM((groups,) + dout.shape, bf16), "d_sent": dma(()),
        "d_came": dma((2, groups // 2 + 1)),
        "dout_turned": pltpu.VMEM((groups, dout.shape[1], tokens), bf16),
        "sums": pltpu.VMEM((8, tokens), f32), "sums_got": pltpu.VMEM((groups, 8, tokens), f32),
        "sum_sems": dma((2,)),
        "grads": pltpu.VMEM((NX, NZ, NC) + piece, f32), "twin_got": pltpu.VMEM((NX, NZ) + piece, f32),
        "mid": pltpu.VMEM((NX, NZ) + piece, f32), "x_got": pltpu.VMEM((2, NZ) + piece, f32), "passing": pltpu.VMEM((2, NZ // 2) + piece, f32),
        "pass_sems": dma((2, 2)),
        "low": pltpu.VMEM((NZ,) + piece, f32), "z_got": pltpu.VMEM((NZ,) + piece, f32),
        "twin_sems": dma((2, NX)), "x_sent": dma(()), "x_came": dma((PARTS, NX)), "z_sent": dma(()),
        "z_came": dma(()),
        "got_b": pltpu.VMEM((groups, share, width), f32), "sum_b": pltpu.VMEM((share, width), f32),
        "b_sems": dma((4,)),
        "got_c": pltpu.VMEM((groups, share, width), f32), "sum_c": pltpu.VMEM((share, width), f32),
        "c_sems": dma((4,)),
    }
    for name in ("fore", "back"):
        scratch |= {
            name + "_state": flat, name + "_came": flat, name + "_twin": half_flat, name + "_half": half_flat,
            name + "_got": slices, name + "_before": slices, name + "_entry": half_flat,
            name + "_give": half_flat, name + "_sems": dma((8,)),
        }
    names = tuple(operands) + tuple(outs) + tuple(scratch)
    vmem = pl.BlockSpec(memory_space=pltpu.VMEM)
    made = pl.pallas_call(
        lambda *refs: whole_kernel(names, *refs),
        out_shape=tuple(outs.values()),
        in_specs=[pl.BlockSpec(memory_space=pltpu.SMEM) if key == "dskip" else vmem for key in operands],
        out_specs=(vmem,) * len(outs),
        scratch_shapes=list(scratch.values()),
        name="whole",
        compiler_params=pltpu.CompilerParams(
            collective_id=0, has_side_effects=True, vmem_limit_bytes=VMEM_LIMIT
        ),
    )(*operands.values())
    anywhere = pl.BlockSpec(memory_space=pl.ANY)
    whole = tuple(outs.values())[:5]
    return pl.pallas_call(
        leave_kernel,
        out_shape=whole + (shape((inner,), f32), shape((heads,), f32)),
        in_specs=[vmem] * 6,
        out_specs=(anywhere,) * 5 + (vmem, pl.BlockSpec(memory_space=pltpu.SMEM)),
        scratch_shapes=[dma((5,))],
        name="leave",
    )(*made)


def solution(mesh):
    return jax.shard_map(
        per_device,
        mesh=mesh,
        in_specs=(
            P("ctx", "head"), P("ctx", "head"), P("ctx", None), P("ctx", None), P("head", "ctx"),
            P("head"), P("head"), P("ctx", "head"), P("ctx", "head"),
        ),
        out_specs=(
            P("ctx", "head"), P("ctx", "head"), P("ctx", None), P("ctx", None), P("ctx", "head"),
            P("head"), P("head"),
        ),
        check_vma=False,
    )
```
